512 devices in a mesh: wide: 128 (over z, x, core), narrow: 4 (over y).
Axes of the slice: x: 4, y: 4, z: 16, core: 2. Of those that a mesh axis runs over, the one named last changes fastest.
Arguments:
- queries: bfloat16 [262144, 1024], P(('wide', 'narrow')), may hold values from -0.25 to 0.25
- responses: bfloat16 [262144, 1024], P(('wide', 'narrow')), may hold values from -0.25 to 0.25
- block_cluster: int32 [2048], replicated, may hold values from 0 to 2047, as said below
Outputs:
- query_loss: float32 [262144], P(('wide', 'narrow'))
- response_loss: float32 [262144], P(('wide', 'narrow'))
- query_grad: bfloat16 [262144, 1024], P(('wide', 'narrow'))
- response_grad: bfloat16 [262144, 1024], P(('wide', 'narrow'))
The draws below stay inside these ranges and needn't reach their ends.
Inputs may be any that keep to these rules, and one draw needn't show every extreme that they name: block_cluster[b] is the first block of b's cluster, so it never falls and is at most b; every aligned group of 4 blocks has a cluster start after its first block, and the first block of every group but the first continues the cluster of the block before it.
All inputs are finite; a program needn't handle non-finite values.
Results may differ from the reference program's by a relative error of at most 0.0065.
Values may be sent and summed in bfloat16 or wider, within the bound.
A program may use at most 64 MiB of HBM per device.

```python
import jax
import jax.numpy as jnp
from jax import lax

D = 1024
BLK = 128
BPD = 4
NB = 2048
NTOT = 262144


def draw_queries(key, part):
    key = jax.random.fold_in(key, 11)
    unit_scale = D ** (-0.5)
    key_main = jax.random.fold_in(key, 0)
    values = jax.random.normal(key_main, (NTOT, D), jnp.float32) * unit_scale
    return jnp.clip(values, -8.0 * unit_scale, 8.0 * unit_scale).astype(jnp.bfloat16)


def draw_responses(key, part):
    key = jax.random.fold_in(key, 23)
    unit_scale = D ** (-0.5)
    key_main = jax.random.fold_in(key, 0)
    values = jax.random.normal(key_main, (NTOT, D), jnp.float32) * unit_scale
    return jnp.clip(values, -8.0 * unit_scale, 8.0 * unit_scale).astype(jnp.bfloat16)


def draw_block_cluster(key, part):
    key = jax.random.fold_in(key, 7)
    devices = NB // BPD
    cut_masks = jax.random.randint(key, (devices,), 1, 2 ** (BPD - 1)).astype(jnp.int32)
    cut_masks = cut_masks.at[devices - 1].set(jnp.bitwise_or(cut_masks[devices - 1], 2 ** (BPD - 2)))
    block_index = jnp.arange(NB).astype(jnp.int32)
    position = block_index % BPD
    group_index = block_index // BPD
    cut_bits = jnp.bitwise_and(jnp.right_shift(cut_masks[group_index], jnp.maximum(position - 1, 0)), 1)
    is_start = jnp.where(position > 0, cut_bits == 1, block_index == 0)
    start_ids = jnp.where(is_start, block_index, 0)
    return lax.cummax(start_ids, axis=0).astype(jnp.int32)


def setup_inputs(seed: int = 0) -> dict:
    streams_of = jax.random.split(jax.random.key(seed), 4)
    queries = draw_queries(jax.random.fold_in(streams_of[3], 71), 0)
    responses = draw_responses(jax.random.fold_in(streams_of[3], 71), 0)
    block_cluster = draw_block_cluster(jax.random.fold_in(streams_of[3], 71), 0)
    return {"queries": queries, "responses": responses, "block_cluster": block_cluster}


logit_scale = 20.0
masked_value = -1.0e30


def block_scores(block_index, block_rows, table, row_ids, block_cluster):
    span_rows = 2 * (BPD - 1) * BLK
    first_row = jnp.minimum(block_cluster[block_index] * BLK, NTOT - span_rows).astype(jnp.int32)
    window_rows = lax.dynamic_slice_in_dim(table, first_row, span_rows, 0)
    window_ids = lax.dynamic_slice_in_dim(row_ids, first_row, span_rows, 0)
    scores = lax.dot_general(block_rows, window_rows, (((1,), (1,)), ((), ())), preferred_element_type=jnp.float32) * logit_scale
    allowed = window_ids[None, :] == block_cluster[block_index]
    return scores, allowed, window_rows, first_row


def log_summed(scores, allowed):
    largest = jnp.max(jnp.where(allowed, scores, masked_value), axis=1)
    summed = jnp.sum(jnp.exp(jnp.where(allowed, scores - largest[:, None], masked_value)), axis=1)
    return largest + jnp.log(summed)


def reference(queries, responses, block_cluster):
    span_rows = 2 * (BPD - 1) * BLK
    row_ids = jnp.repeat(block_cluster, BLK, total_repeat_length=NTOT).astype(jnp.int32)
    query_blocks = queries.reshape(NB, BLK, D)
    response_blocks = responses.reshape(NB, BLK, D)
    indices = jnp.arange(NB).astype(jnp.int32)

    def row_part(inputs):
        block_index, block_rows = inputs
        scores, allowed, window_rows, first_row = block_scores(block_index, block_rows, responses, row_ids, block_cluster)
        return log_summed(scores, allowed)

    def col_part(inputs):
        block_index, block_rows = inputs
        scores, allowed, window_rows, first_row = block_scores(block_index, block_rows, queries, row_ids, block_cluster)
        return log_summed(scores, allowed)

    lse_rows = lax.map(row_part, (indices, query_blocks)).reshape(NTOT)
    lse_cols = lax.map(col_part, (indices, response_blocks)).reshape(NTOT)
    diagonal = jnp.sum(queries.astype(jnp.float32) * responses.astype(jnp.float32), axis=1) * logit_scale
    query_loss = lse_rows - diagonal
    response_loss = lse_cols - diagonal

    def identity_part(block_index, first_row):
        columns = (first_row + jnp.arange(span_rows).astype(jnp.int32))[None, :]
        own_rows = (block_index * BLK + jnp.arange(BLK).astype(jnp.int32))[:, None]
        return (columns == own_rows).astype(jnp.float32)

    def query_part(inputs):
        block_index, block_rows = inputs
        scores, allowed, window_rows, first_row = block_scores(block_index, block_rows, responses, row_ids, block_cluster)
        own_lse = lax.dynamic_slice_in_dim(lse_rows, (block_index * BLK).astype(jnp.int32), BLK)
        window_lse = lax.dynamic_slice_in_dim(lse_cols, first_row, span_rows)
        weights = jnp.where(allowed, jnp.exp(scores - own_lse[:, None]) + jnp.exp(scores - window_lse[None, :]), 0.0)
        weights = (weights - 2.0 * identity_part(block_index, first_row)).astype(jnp.bfloat16)
        return jnp.dot(weights, window_rows, preferred_element_type=jnp.float32) * logit_scale

    def response_part(inputs):
        block_index, block_rows = inputs
        scores, allowed, window_rows, first_row = block_scores(block_index, block_rows, queries, row_ids, block_cluster)
        own_lse = lax.dynamic_slice_in_dim(lse_cols, (block_index * BLK).astype(jnp.int32), BLK)
        window_lse = lax.dynamic_slice_in_dim(lse_rows, first_row, span_rows)
        weights = jnp.where(allowed, jnp.exp(scores - window_lse[None, :]) + jnp.exp(scores - own_lse[:, None]), 0.0)
        weights = (weights - 2.0 * identity_part(block_index, first_row)).astype(jnp.bfloat16)
        return jnp.dot(weights, window_rows, preferred_element_type=jnp.float32) * logit_scale

    query_grad = lax.map(query_part, (indices, query_blocks)).reshape(NTOT, D).astype(jnp.bfloat16)
    response_grad = lax.map(response_part, (indices, response_blocks)).reshape(NTOT, D).astype(jnp.bfloat16)
    return query_loss, response_loss, query_grad, response_grad
```

```python
import jax
import jax.numpy as jnp
from jax import lax
from jax.experimental import pallas as pl
from jax.experimental.pallas import tpu as pltpu
from jax.sharding import PartitionSpec as P

MESH = pl.DeviceIdType.MESH
BLK = 128
ROWS = 512
D = 1024
HALF = 64
CHUNKS = 6
DEPTH = 3
SCALE = 20.0
MASKED = -1e30
F32 = jnp.float32
BF16 = jnp.bfloat16
BLOCKS = ROWS // BLK


def dot_rows(former, latter):
    return lax.dot_general(former, latter, (((1,), (1,)), ((), ())), preferred_element_type=F32)


def dot(former, latter):
    return jnp.dot(former, latter, preferred_element_type=F32)


def rows_of(b):
    return pl.ds(b * BLK, BLK)


def lanes(shape):
    return lax.broadcasted_iota(jnp.int32, shape, len(shape) - 1)


def eye():
    shape = (BLK, BLK)
    return lax.broadcasted_iota(jnp.int32, shape, 0) == lanes(shape)


def to_lanes(column):
    return jnp.sum(jnp.where(eye(), column, 0.0), axis=0, keepdims=True)


def wide(column):
    return jnp.broadcast_to(column[:, :1], (BLK, D))


def exchange(
    q_hbm, r_hbm, cluster_hbm,
    g1, g2, h1, e_own, r_own, m_col, z_col, m_first, bias, last_msg, last_q, loss_q, diag_out,
    q_own, held, s_own, t_own, x_ref, h2, m_row, z_row, msg_right, msg_left, got_left, got_right, ids,
    send_sem, recv_sem, msg_send, msg_recv, load_sem,
):
    shape_wide, shape_narrow = lax.axis_size("wide"), lax.axis_size("narrow")
    count = shape_wide * shape_narrow
    me = lax.axis_index("wide") * shape_narrow + lax.axis_index("narrow")
    left, right = lax.rem(me + count - 1, count), lax.rem(me + 1, count)

    def coords(p):
        return (p // shape_narrow, lax.rem(p, shape_narrow))

    loads = [
        pltpu.make_async_copy(q_hbm, q_own, load_sem.at[0]),
        pltpu.make_async_copy(r_hbm, r_own, load_sem.at[1]),
        pltpu.make_async_copy(cluster_hbm, ids, load_sem.at[2]),
    ]
    for load in loads:
        load.start()

    barrier = pltpu.get_barrier_semaphore()
    for p in (left, right):
        pl.semaphore_signal(barrier, inc=1, device_id=coords(p), device_id_type=MESH)
    pl.semaphore_wait(barrier, 2)

    def copies(src, slot, c):
        to_right = pltpu.make_async_remote_copy(
            src_ref=src.at[pl.ds(BLK + c * HALF, HALF)],
            dst_ref=held.at[slot, pl.ds(0, HALF)],
            send_sem=send_sem.at[slot, 0],
            recv_sem=recv_sem.at[slot, 0],
            device_id=coords(right),
            device_id_type=MESH,
        )
        to_left = pltpu.make_async_remote_copy(
            src_ref=src.at[pl.ds(c * HALF, HALF)],
            dst_ref=held.at[slot, pl.ds(HALF, HALF)],
            send_sem=send_sem.at[slot, 1],
            recv_sem=recv_sem.at[slot, 1],
            device_id=coords(left),
            device_id_type=MESH,
        )
        return to_right, to_left

    def start(src, slot, c):
        for copy in copies(src, slot, c):
            copy.start()

    def sent(src, slot, c):
        for copy in copies(src, slot, c):
            copy.wait_send()

    def landed(src, slot, c):
        for copy in copies(src, slot, c):
            copy.wait_recv()

    for c in range(DEPTH):
        start(r_hbm, c, c)

    for load in loads:
        load.wait()
    own_ids = [ids[me * BLOCKS + b] for b in range(BLOCKS)]
    lane = lanes((1, ROWS))
    id_row = jnp.full((1, ROWS), own_ids[0], jnp.int32)
    for b in range(1, BLOCKS):
        id_row = jnp.where(lane >= b * BLK, own_ids[b], id_row)

    for b in range(BLOCKS):
        allowed = jnp.broadcast_to(id_row == own_ids[b], (BLK, ROWS))
        s_own[rows_of(b)] = jnp.where(allowed, dot_rows(q_own[rows_of(b)], r_own[...]) * SCALE, MASKED)
        t_own[rows_of(b)] = jnp.where(allowed, dot_rows(r_own[rows_of(b)], q_own[...]) * SCALE, MASKED)

    def sums_by_lane(scores):
        largest = jnp.max(scores[...], axis=0, keepdims=True)
        return largest, jnp.sum(jnp.exp(scores[...] - largest), axis=0, keepdims=True)

    largest_cols, summed_cols = sums_by_lane(s_own)
    largest_rows, summed_rows = sums_by_lane(t_own)
    for k, lse in enumerate((largest_cols + jnp.log(summed_cols), largest_rows + jnp.log(summed_rows))):
        lse = jnp.broadcast_to(lse, (8, ROWS))
        ahead, behind = pltpu.roll(lse, ROWS - HALF, 1), pltpu.roll(lse, HALF, 1)
        for c in range(CHUNKS):
            at = (c // 2) * BLK
            row = pl.ds(8 * k + c, 1)
            msg_right[row] = (ahead if c % 2 else lse)[:1, BLK + at : 2 * BLK + at]
            msg_left[row] = (lse if c % 2 else behind)[:1, at : BLK + at]
        rest = pl.ds(8 * k + CHUNKS, 8 - CHUNKS)
        msg_right[rest] = jnp.zeros((8 - CHUNKS, BLK), F32)
        msg_left[rest] = jnp.zeros((8 - CHUNKS, BLK), F32)
    messages = [
        pltpu.make_async_remote_copy(
            src_ref=src,
            dst_ref=dst,
            send_sem=msg_send.at[k],
            recv_sem=msg_recv.at[k],
            device_id=coords(p),
            device_id_type=MESH,
        )
        for k, (src, dst, p) in enumerate(((msg_right, got_left, right), (msg_left, got_right, left)))
    ]
    for message in messages:
        message.start()

    def own_part(scores, other, m_ref, z_ref, total):
        for b in range(BLOCKS):
            x = scores[rows_of(b)]
            largest = jnp.max(x, axis=1, keepdims=True)
            e = jnp.exp(x - largest)
            m_ref[rows_of(b)] = jnp.broadcast_to(largest, (BLK, BLK))
            z_ref[rows_of(b)] = jnp.broadcast_to(jnp.sum(e, axis=1, keepdims=True), (BLK, BLK))
            total[rows_of(b)] = dot(e.astype(BF16), other[...])

    own_part(s_own, r_own, m_row, z_row, h1)
    own_part(t_own, q_own, m_col, z_col, g1)
    e_own[...] = jnp.exp(s_own[...] - largest_cols)
    m_first[...] = jnp.broadcast_to(largest_cols, (8, ROWS))
    h2[...] = jnp.zeros_like(h2)

    first_half = lanes((1, BLK)) < HALF

    def ids_of(c):
        return jnp.where(first_half, ids[left * BLOCKS + 1 + c // 2], ids[right * BLOCKS + c // 2])

    def message_of(row):
        return jnp.where(first_half, got_left[pl.ds(row, 1)], got_right[pl.ds(row, 1)])

    def chunk_part(c, slot, msg_row, own, m_ref, z_ref, scaled, total):
        chunk = held.at[slot]
        id_chunk = ids_of(c)
        for b in range(BLOCKS):
            allowed = jnp.broadcast_to(id_chunk == own_ids[b], (BLK, BLK))
            x_ref[rows_of(b)] = jnp.where(allowed, dot_rows(own[rows_of(b)], chunk[...]) * SCALE, MASKED)
        msg = message_of(msg_row)
        largest = jnp.maximum(jnp.max(x_ref[...], axis=0, keepdims=True), msg)
        summed = jnp.exp(msg - largest) + jnp.sum(jnp.exp(x_ref[...] - largest), axis=0, keepdims=True)
        lse = largest + jnp.log(summed)
        for b in range(BLOCKS):
            rows = rows_of(b)
            x = x_ref[rows]
            before = m_ref[rows]
            after = jnp.maximum(before, jnp.max(x, axis=1, keepdims=True))
            shrink = jnp.exp(before - after)
            e = jnp.exp(x - after)
            m_ref[rows] = after
            z_ref[rows] = z_ref[rows] * shrink + jnp.sum(e, axis=1, keepdims=True)
            scaled[rows] = scaled[rows] * wide(shrink) + dot(e.astype(BF16), chunk[...])
            total[rows] += dot(jnp.exp(x - lse).astype(BF16), chunk[...])

    for message in messages:
        message.wait()

    @pl.loop(0, CHUNKS)
    def _(c):
        sent(r_hbm, c, c)

        @pl.when(c < CHUNKS - DEPTH)
        def _():
            start(r_hbm, c + DEPTH, c + DEPTH)

        @pl.when(c >= CHUNKS - DEPTH)
        def _():
            start(q_hbm, c + DEPTH, c + DEPTH - CHUNKS)

        landed(r_hbm, c, c)
        chunk_part(c, c, c, q_own, m_row, z_row, h1, h2)

    row_lse = []
    diagonal = []
    for b in range(BLOCKS):
        rows = rows_of(b)
        z = z_row[rows]
        row_lse.append(to_lanes(m_row[rows] + jnp.log(z)))
        diagonal.append(to_lanes(s_own[rows, b * BLK : (b + 1) * BLK]))
        h1[rows] = h1[rows] * wide(1.0 / z) + h2[rows] - r_own[rows].astype(F32)
        loss_q[pl.ds(b, 1)] = row_lse[b] - diagonal[b]
        diag_out[pl.ds(b, 1)] = diagonal[b]
    row_lse = jnp.concatenate(row_lse, axis=1)
    for b in range(BLOCKS):
        rows = rows_of(b)
        at_diagonal = lanes((BLK, ROWS)) == lax.broadcasted_iota(jnp.int32, (BLK, ROWS), 0) + b * BLK
        w = jnp.exp(t_own[rows] - row_lse) - jnp.where(at_diagonal, 1.0, 0.0)
        g2[rows] = dot(w.astype(BF16), q_own[...]) - q_own[rows].astype(F32)

    @pl.loop(0, CHUNKS - 1)
    def _(c):
        sent(q_hbm, CHUNKS + c, c)

        @pl.when(c < CHUNKS - DEPTH)
        def _():
            start(q_hbm, CHUNKS + c + DEPTH, c + DEPTH)

        landed(q_hbm, CHUNKS + c, c)
        chunk_part(c, CHUNKS + c, 8 + c, r_own, m_col, z_col, g1, g2)

    c = CHUNKS - 1
    id_chunk = ids_of(c)
    for b in range(BLOCKS):
        allowed = jnp.broadcast_to(id_chunk == own_ids[b], (BLK, BLK))
        bias[rows_of(b)] = jnp.where(allowed, 0.0, MASKED)
    last_msg[...] = jnp.broadcast_to(message_of(8 + c), (8, BLK))
    sent(q_hbm, CHUNKS + c, c)
    landed(q_hbm, CHUNKS + c, c)
    last_q[...] = held[CHUNKS + c]


def finish(
    g1, g2, h1, e_own, r_own, m_col, z_col, m_first, bias, last_msg, last_q, loss_q, diagonal,
    loss_q_out, loss_r_out, q_out, r_out,
    x_ref, w_ref, gq, gr, sems,
):
    for b in range(BLOCKS):
        rows = rows_of(b)
        x = dot_rows(r_own[rows], last_q[...]) * SCALE
        x_ref[rows] = jnp.where(bias[rows] < 0.0, MASKED, x)
    msg = last_msg[:1]
    largest = jnp.maximum(jnp.max(x_ref[...], axis=0, keepdims=True), msg)
    summed = jnp.exp(msg - largest) + jnp.sum(jnp.exp(x_ref[...] - largest), axis=0, keepdims=True)
    row_lse = largest + jnp.log(summed)
    loss_q_out[...] = loss_q[...]
    factors = []
    copies = []
    for b in range(BLOCKS):
        rows = rows_of(b)
        x = x_ref[rows]
        before = m_col[rows]
        after = jnp.maximum(before, jnp.max(x, axis=1, keepdims=True))
        shrink = jnp.exp(before - after)
        e = jnp.exp(x - after)
        z = z_col[rows] * shrink + jnp.sum(e, axis=1, keepdims=True)
        inverse = 1.0 / z
        col_lse = to_lanes(after + jnp.log(z))
        loss_r_out[pl.ds(b, 1)] = col_lse - diagonal[pl.ds(b, 1)]
        factors.append(jnp.exp(m_first[:1, b * BLK : (b + 1) * BLK] - col_lse))
        w = e * inverse + jnp.exp(x - row_lse)
        total = g1[rows] * wide(shrink * inverse) + g2[rows] + dot(w.astype(BF16), last_q[...])
        gr[rows] = (total * SCALE).astype(BF16)
        copies.append(pltpu.make_async_copy(gr.at[rows], r_out.at[rows], sems.at[b]))
        copies[-1].start()
    factors = jnp.concatenate(factors, axis=1)
    for b in range(BLOCKS):
        rows = rows_of(b)
        at_diagonal = lanes((BLK, ROWS)) == lax.broadcasted_iota(jnp.int32, (BLK, ROWS), 0) + b * BLK
        w = e_own[rows] * factors - jnp.where(at_diagonal, 1.0, 0.0)
        total = h1[rows] + dot(w.astype(BF16), r_own[...])
        gq[rows] = (total * SCALE).astype(BF16)
        copies.append(pltpu.make_async_copy(gq.at[rows], q_out.at[rows], sems.at[BLOCKS + b]))
        copies[-1].start()
    for copy in copies:
        copy.wait()


def shards(queries, responses, block_cluster):
    queries, responses, block_cluster = (
        pltpu.with_memory_space_constraint(a, pltpu.HBM) for a in (queries, responses, block_cluster)
    )
    vmem = pl.BlockSpec(memory_space=pltpu.VMEM)
    hbm = pl.BlockSpec(memory_space=pltpu.HBM)
    passed = (
        ((ROWS, D), F32),
        ((ROWS, D), F32),
        ((ROWS, D), F32),
        ((ROWS, ROWS), F32),
        ((ROWS, D), BF16),
        ((ROWS, BLK), F32),
        ((ROWS, BLK), F32),
        ((8, ROWS), F32),
        ((ROWS, BLK), F32),
        ((8, BLK), F32),
        ((BLK, D), BF16),
        ((BLOCKS, BLK), F32),
        ((BLOCKS, BLK), F32),
    )
    parts = pl.pallas_call(
        exchange,
        out_shape=[pltpu.VMEM(shape, dtype) for shape, dtype in passed],
        in_specs=[hbm] * 3,
        out_specs=[vmem] * len(passed),
        scratch_shapes=[
            pltpu.VMEM((ROWS, D), BF16),
            pltpu.VMEM((2 * CHUNKS, BLK, D), BF16),
            pltpu.VMEM((ROWS, ROWS), F32),
            pltpu.VMEM((ROWS, ROWS), F32),
            pltpu.VMEM((ROWS, BLK), F32),
            pltpu.VMEM((ROWS, D), F32),
            pltpu.VMEM((ROWS, BLK), F32),
            pltpu.VMEM((ROWS, BLK), F32),
            pltpu.VMEM((16, BLK), F32),
            pltpu.VMEM((16, BLK), F32),
            pltpu.VMEM((16, BLK), F32),
            pltpu.VMEM((16, BLK), F32),
            pltpu.SMEM(block_cluster.shape, jnp.int32),
            pltpu.SemaphoreType.DMA((2 * CHUNKS, 2)),
            pltpu.SemaphoreType.DMA((2 * CHUNKS, 2)),
            pltpu.SemaphoreType.DMA((2,)),
            pltpu.SemaphoreType.DMA((2,)),
            pltpu.SemaphoreType.DMA((3,)),
        ],
        compiler_params=pltpu.CompilerParams(
            collective_id=0, has_side_effects=True, vmem_limit_bytes=32 * 2**20
        ),
        name="exchange",
    )(queries, responses, block_cluster)
    query_loss, response_loss, query_grad, response_grad = pl.pallas_call(
        finish,
        out_shape=[
            jax.ShapeDtypeStruct((BLOCKS, BLK), F32),
            jax.ShapeDtypeStruct((BLOCKS, BLK), F32),
            jax.ShapeDtypeStruct((ROWS, D), BF16),
            jax.ShapeDtypeStruct((ROWS, D), BF16),
        ],
        in_specs=[vmem] * len(passed),
        out_specs=[vmem, vmem, hbm, hbm],
        scratch_shapes=[
            pltpu.VMEM((ROWS, BLK), F32),
            pltpu.VMEM((ROWS, BLK), BF16),
            pltpu.VMEM((ROWS, D), BF16),
            pltpu.VMEM((ROWS, D), BF16),
            pltpu.SemaphoreType.DMA((2 * BLOCKS,)),
        ],
        compiler_params=pltpu.CompilerParams(vmem_limit_bytes=32 * 2**20),
        name="finish",
    )(*parts)
    return query_loss.reshape(ROWS), response_loss.reshape(ROWS), query_grad, response_grad


def solution(mesh):
    both = ("wide", "narrow")
    return jax.shard_map(
        shards,
        mesh=mesh,
        in_specs=(P(both, None), P(both, None), P()),
        out_specs=(P(both), P(both), P(both, None), P(both, None)),
        check_vma=False,
    )
```

```python
import jax
import jax.numpy as jnp
from jax import lax
from jax.experimental import pallas as pl
from jax.experimental.pallas import tpu as pltpu
from jax.sharding import PartitionSpec as P

MESH = pl.DeviceIdType.MESH
BLK = 128
ROWS = 512
D = 1024
HALF = 64
CHUNKS = 6
SCALE = 20.0
MASKED = -1e30
F32 = jnp.float32
BF16 = jnp.bfloat16
BLOCKS = ROWS // BLK


def dot_rows(former, latter):
    return lax.dot_general(former, latter, (((1,), (1,)), ((), ())), preferred_element_type=F32)


def dot(former, latter):
    return jnp.dot(former, latter, preferred_element_type=F32)


def rows_of(b):
    return pl.ds(b * BLK, BLK)


def lanes(shape):
    return lax.broadcasted_iota(jnp.int32, shape, len(shape) - 1)


def eye():
    shape = (BLK, BLK)
    return lax.broadcasted_iota(jnp.int32, shape, 0) == lanes(shape)


def to_lanes(column):
    return jnp.sum(jnp.where(eye(), column, 0.0), axis=0, keepdims=True)


def wide(column):
    return jnp.broadcast_to(column[:, :1], (BLK, D))


def exchange(
    q_hbm, r_hbm, cluster_hbm,
    g1, g2, h1, e_own, r_own, m_col, z_col, m_first, bias, last_msg, last_q, loss_q, diag_out,
    q_own, held, s_own, t_own, x_ref, msg_right, msg_left, got_left, got_right, ids,
    send_sem, recv_sem, msg_send, msg_recv, load_sem,
):
    shape_wide, shape_narrow = lax.axis_size("wide"), lax.axis_size("narrow")
    count = shape_wide * shape_narrow
    me = lax.axis_index("wide") * shape_narrow + lax.axis_index("narrow")
    left, right = lax.rem(me + count - 1, count), lax.rem(me + 1, count)

    def coords(p):
        return (p // shape_narrow, lax.rem(p, shape_narrow))

    loads = [
        pltpu.make_async_copy(q_hbm, q_own, load_sem.at[0]),
        pltpu.make_async_copy(r_hbm, r_own, load_sem.at[1]),
        pltpu.make_async_copy(cluster_hbm, ids, load_sem.at[2]),
    ]
    for load in loads:
        load.start()

    barrier = pltpu.get_barrier_semaphore()
    for p in (left, right):
        pl.semaphore_signal(barrier, inc=1, device_id=coords(p), device_id_type=MESH)
    pl.semaphore_wait(barrier, 2)

    def copies(src, slot, c):
        to_right = pltpu.make_async_remote_copy(
            src_ref=src.at[pl.ds(BLK + c * HALF, HALF)],
            dst_ref=held.at[slot, pl.ds(0, HALF)],
            send_sem=send_sem.at[slot, 0],
            recv_sem=recv_sem.at[slot, 0],
            device_id=coords(right),
            device_id_type=MESH,
        )
        to_left = pltpu.make_async_remote_copy(
            src_ref=src.at[pl.ds(c * HALF, HALF)],
            dst_ref=held.at[slot, pl.ds(HALF, HALF)],
            send_sem=send_sem.at[slot, 1],
            recv_sem=recv_sem.at[slot, 1],
            device_id=coords(left),
            device_id_type=MESH,
        )
        return to_right, to_left

    def start(src, slot, c):
        for copy in copies(src, slot, c):
            copy.start()

    def landed(src, slot, c):
        for copy in copies(src, slot, c):
            copy.wait_recv()

    for c in range(CHUNKS):
        start(r_hbm, c, c)

    for load in loads:
        load.wait()
    own_ids = [ids[me * BLOCKS + b] for b in range(BLOCKS)]
    lane = lanes((1, ROWS))
    id_row = jnp.full((1, ROWS), own_ids[0], jnp.int32)
    for b in range(1, BLOCKS):
        id_row = jnp.where(lane >= b * BLK, own_ids[b], id_row)

    for b in range(BLOCKS):
        allowed = jnp.broadcast_to(id_row == own_ids[b], (BLK, ROWS))
        s_own[rows_of(b)] = jnp.where(allowed, dot_rows(q_own[rows_of(b)], r_own[...]) * SCALE, MASKED)
        t_own[rows_of(b)] = jnp.where(allowed, dot_rows(r_own[rows_of(b)], q_own[...]) * SCALE, MASKED)

    def sums_by_lane(scores):
        largest = jnp.max(scores[...], axis=0, keepdims=True)
        return largest, jnp.sum(jnp.exp(scores[...] - largest), axis=0, keepdims=True)

    largest_cols, summed_cols = sums_by_lane(s_own)
    largest_rows, summed_rows = sums_by_lane(t_own)
    for k, lse in enumerate((largest_cols + jnp.log(summed_cols), largest_rows + jnp.log(summed_rows))):
        lse = jnp.broadcast_to(lse, (8, ROWS))
        ahead, behind = pltpu.roll(lse, ROWS - HALF, 1), pltpu.roll(lse, HALF, 1)
        for c in range(CHUNKS):
            at = (c // 2) * BLK
            row = pl.ds(8 * k + c, 1)
            msg_right[row] = (ahead if c % 2 else lse)[:1, BLK + at : 2 * BLK + at]
            msg_left[row] = (lse if c % 2 else behind)[:1, at : BLK + at]
        rest = pl.ds(8 * k + CHUNKS, 8 - CHUNKS)
        msg_right[rest] = jnp.zeros((8 - CHUNKS, BLK), F32)
        msg_left[rest] = jnp.zeros((8 - CHUNKS, BLK), F32)
    messages = [
        pltpu.make_async_remote_copy(
            src_ref=src,
            dst_ref=dst,
            send_sem=msg_send.at[k],
            recv_sem=msg_recv.at[k],
            device_id=coords(p),
            device_id_type=MESH,
        )
        for k, (src, dst, p) in enumerate(((msg_right, got_left, right), (msg_left, got_right, left)))
    ]
    for message in messages:
        message.start()
    for c in range(CHUNKS):
        start(q_hbm, CHUNKS + c, c)

    for b in range(BLOCKS):
        rows = rows_of(b)
        x = t_own[rows]
        largest = jnp.max(x, axis=1, keepdims=True)
        e = jnp.exp(x - largest)
        m_col[rows] = jnp.broadcast_to(largest, (BLK, BLK))
        z_col[rows] = jnp.broadcast_to(jnp.sum(e, axis=1, keepdims=True), (BLK, BLK))
        g1[rows] = dot(e.astype(BF16), q_own[...])
    e_own[...] = jnp.exp(s_own[...] - largest_cols)
    m_first[...] = jnp.broadcast_to(largest_cols, (8, ROWS))

    first_half = lanes((1, BLK)) < HALF

    def ids_of(c):
        return jnp.where(first_half, ids[left * BLOCKS + 1 + c // 2], ids[right * BLOCKS + c // 2])

    def scores_of(c, slot, own):
        id_chunk = ids_of(c)
        for b in range(BLOCKS):
            allowed = jnp.broadcast_to(id_chunk == own_ids[b], (BLK, BLK))
            x_ref[c, rows_of(b)] = jnp.where(allowed, dot_rows(own[rows_of(b)], held[slot]) * SCALE, MASKED)

    def lse_of(c, msg_row):
        x = x_ref[c]
        msg = jnp.where(first_half, got_left[pl.ds(msg_row, 1)], got_right[pl.ds(msg_row, 1)])
        largest = jnp.maximum(jnp.max(x, axis=0, keepdims=True), msg)
        summed = jnp.exp(msg - largest) + jnp.sum(jnp.exp(x - largest), axis=0, keepdims=True)
        return largest + jnp.log(summed)

    def at_diagonal(b):
        shape = (BLK, ROWS)
        return lanes(shape) == lax.broadcasted_iota(jnp.int32, shape, 0) + b * BLK

    @pl.loop(0, CHUNKS)
    def _(c):
        landed(r_hbm, c, c)
        scores_of(c, c, q_own)

    for message in messages:
        message.wait()
    col_lse = jnp.concatenate([lse_of(c, c) for c in range(CHUNKS)], axis=1)
    row_lse = []
    for b in range(BLOCKS):
        rows = rows_of(b)
        own = s_own[rows]
        others = jnp.concatenate([x_ref[c, rows] for c in range(CHUNKS)], axis=1)
        largest = jnp.maximum(jnp.max(own, axis=1, keepdims=True), jnp.max(others, axis=1, keepdims=True))
        summed = jnp.sum(jnp.exp(own - largest), axis=1, keepdims=True)
        summed += jnp.sum(jnp.exp(others - largest), axis=1, keepdims=True)
        lse = largest + jnp.log(summed)
        w_own = jnp.exp(own - lse) - jnp.where(at_diagonal(b), 1.0, 0.0)
        w_others = jnp.exp(others - lse) + jnp.exp(others - col_lse)
        h1[rows] = dot(w_own.astype(BF16), r_own[...]) + dot(
            w_others.astype(BF16), held[:CHUNKS].reshape(CHUNKS * BLK, D)
        )
        row_lse.append(to_lanes(lse))
        diagonal = to_lanes(s_own[rows, b * BLK : (b + 1) * BLK])
        loss_q[pl.ds(b, 1)] = row_lse[b] - diagonal
        diag_out[pl.ds(b, 1)] = diagonal
    row_lse = jnp.concatenate(row_lse, axis=1)
    for b in range(BLOCKS):
        rows = rows_of(b)
        w = jnp.exp(t_own[rows] - row_lse) - jnp.where(at_diagonal(b), 1.0, 0.0)
        g2[rows] = dot(w.astype(BF16), q_own[...]) - q_own[rows].astype(F32)

    for first, end in ((0, CHUNKS // 2), (CHUNKS // 2, CHUNKS - 1)):

        @pl.loop(first, end)
        def _(c):
            landed(q_hbm, CHUNKS + c, c)
            scores_of(c, CHUNKS + c, r_own)

        group = range(first, end)
        lse = jnp.concatenate([lse_of(c, 8 + c) for c in group], axis=1)
        for b in range(BLOCKS):
            rows = rows_of(b)
            x = jnp.concatenate([x_ref[c, rows] for c in group], axis=1)
            before = m_col[rows]
            after = jnp.maximum(before, jnp.max(x, axis=1, keepdims=True))
            shrink = jnp.exp(before - after)
            e = jnp.exp(x - after[:, :1])
            m_col[rows] = after
            z_col[rows] = z_col[rows] * shrink + jnp.sum(e, axis=1, keepdims=True)
            queries = held[CHUNKS + first : CHUNKS + end].reshape(len(group) * BLK, D)
            g1[rows] = g1[rows] * wide(shrink) + dot(e.astype(BF16), queries)
            g2[rows] += dot(jnp.exp(x - lse).astype(BF16), queries)

    c = CHUNKS - 1
    id_chunk = ids_of(c)
    for b in range(BLOCKS):
        allowed = jnp.broadcast_to(id_chunk == own_ids[b], (BLK, BLK))
        bias[rows_of(b)] = jnp.where(allowed, 0.0, MASKED)
    row = pl.ds(8 + c, 1)
    last_msg[...] = jnp.broadcast_to(jnp.where(first_half, got_left[row], got_right[row]), (8, BLK))
    landed(q_hbm, CHUNKS + c, c)
    last_q[...] = held[CHUNKS + c]
    for c in range(CHUNKS):
        for src, slot in ((r_hbm, c), (q_hbm, CHUNKS + c)):
            for copy in copies(src, slot, c):
                copy.wait_send()


def finish(
    g1, g2, h1, e_own, r_own, m_col, z_col, m_first, bias, last_msg, last_q, loss_q, diagonal,
    loss_q_out, loss_r_out, q_out, r_out,
    x_ref, gq, gr, sems,
):
    for b in range(BLOCKS):
        rows = rows_of(b)
        x = dot_rows(r_own[rows], last_q[...]) * SCALE
        x_ref[rows] = jnp.where(bias[rows] < 0.0, MASKED, x)
    msg = last_msg[:1]
    largest = jnp.maximum(jnp.max(x_ref[...], axis=0, keepdims=True), msg)
    summed = jnp.exp(msg - largest) + jnp.sum(jnp.exp(x_ref[...] - largest), axis=0, keepdims=True)
    row_lse = largest + jnp.log(summed)
    loss_q_out[...] = loss_q[...]
    factors = []
    copies = []
    for b in range(BLOCKS):
        rows = rows_of(b)
        x = x_ref[rows]
        before = m_col[rows]
        after = jnp.maximum(before, jnp.max(x, axis=1, keepdims=True))
        shrink = jnp.exp(before - after)
        e = jnp.exp(x - after)
        z = z_col[rows] * shrink + jnp.sum(e, axis=1, keepdims=True)
        inverse = 1.0 / z
        col_lse = to_lanes(after + jnp.log(z))
        loss_r_out[pl.ds(b, 1)] = col_lse - diagonal[pl.ds(b, 1)]
        factors.append(jnp.exp(m_first[:1, b * BLK : (b + 1) * BLK] - col_lse))
        w = e * inverse + jnp.exp(x - row_lse)
        total = g1[rows] * wide(shrink * inverse) + g2[rows] + dot(w.astype(BF16), last_q[...])
        gr[rows] = (total * SCALE).astype(BF16)
        copies.append(pltpu.make_async_copy(gr.at[rows], r_out.at[rows], sems.at[b]))
        copies[-1].start()
    factors = jnp.concatenate(factors, axis=1)
    for b in range(BLOCKS):
        rows = rows_of(b)
        at_diagonal = lanes((BLK, ROWS)) == lax.broadcasted_iota(jnp.int32, (BLK, ROWS), 0) + b * BLK
        w = e_own[rows] * factors - jnp.where(at_diagonal, 1.0, 0.0)
        total = h1[rows] + dot(w.astype(BF16), r_own[...])
        gq[rows] = (total * SCALE).astype(BF16)
        copies.append(pltpu.make_async_copy(gq.at[rows], q_out.at[rows], sems.at[BLOCKS + b]))
        copies[-1].start()
    for copy in copies:
        copy.wait()


def shards(queries, responses, block_cluster):
    queries, responses, block_cluster = (
        pltpu.with_memory_space_constraint(a, pltpu.HBM) for a in (queries, responses, block_cluster)
    )
    vmem = pl.BlockSpec(memory_space=pltpu.VMEM)
    hbm = pl.BlockSpec(memory_space=pltpu.HBM)
    passed = (
        ((ROWS, D), F32),
        ((ROWS, D), F32),
        ((ROWS, D), F32),
        ((ROWS, ROWS), F32),
        ((ROWS, D), BF16),
        ((ROWS, BLK), F32),
        ((ROWS, BLK), F32),
        ((8, ROWS), F32),
        ((ROWS, BLK), F32),
        ((8, BLK), F32),
        ((BLK, D), BF16),
        ((BLOCKS, BLK), F32),
        ((BLOCKS, BLK), F32),
    )
    parts = pl.pallas_call(
        exchange,
        out_shape=[pltpu.VMEM(shape, dtype) for shape, dtype in passed],
        in_specs=[hbm] * 3,
        out_specs=[vmem] * len(passed),
        scratch_shapes=[
            pltpu.VMEM((ROWS, D), BF16),
            pltpu.VMEM((2 * CHUNKS, BLK, D), BF16),
            pltpu.VMEM((ROWS, ROWS), F32),
            pltpu.VMEM((ROWS, ROWS), F32),
            pltpu.VMEM((CHUNKS, ROWS, BLK), F32),
            pltpu.VMEM((16, BLK), F32),
            pltpu.VMEM((16, BLK), F32),
            pltpu.VMEM((16, BLK), F32),
            pltpu.VMEM((16, BLK), F32),
            pltpu.SMEM(block_cluster.shape, jnp.int32),
            pltpu.SemaphoreType.DMA((2 * CHUNKS, 2)),
            pltpu.SemaphoreType.DMA((2 * CHUNKS, 2)),
            pltpu.SemaphoreType.DMA((2,)),
            pltpu.SemaphoreType.DMA((2,)),
            pltpu.SemaphoreType.DMA((3,)),
        ],
        compiler_params=pltpu.CompilerParams(
            collective_id=0, has_side_effects=True, vmem_limit_bytes=32 * 2**20
        ),
        name="exchange",
    )(queries, responses, block_cluster)
    query_loss, response_loss, query_grad, response_grad = pl.pallas_call(
        finish,
        out_shape=[
            jax.ShapeDtypeStruct((BLOCKS, BLK), F32),
            jax.ShapeDtypeStruct((BLOCKS, BLK), F32),
            jax.ShapeDtypeStruct((ROWS, D), BF16),
            jax.ShapeDtypeStruct((ROWS, D), BF16),
        ],
        in_specs=[vmem] * len(passed),
        out_specs=[vmem, vmem, hbm, hbm],
        scratch_shapes=[
            pltpu.VMEM((ROWS, BLK), F32),
            pltpu.VMEM((ROWS, D), BF16),
            pltpu.VMEM((ROWS, D), BF16),
            pltpu.SemaphoreType.DMA((2 * BLOCKS,)),
        ],
        compiler_params=pltpu.CompilerParams(vmem_limit_bytes=32 * 2**20),
        name="finish",
    )(*parts)
    return query_loss.reshape(ROWS), response_loss.reshape(ROWS), query_grad, response_grad


def solution(mesh):
    both = ("wide", "narrow")
    return jax.shard_map(
        shards,
        mesh=mesh,
        in_specs=(P(both, None), P(both, None), P()),
        out_specs=(P(both), P(both), P(both, None), P(both, None)),
        check_vma=False,
    )
```

```python
import math

import jax
import jax.numpy as jnp
from jax import lax
from jax.experimental import pallas as pl
from jax.experimental.pallas import tpu as pltpu
from jax.sharding import PartitionSpec as P

MESH = pl.DeviceIdType.MESH
BLK = 128
ROWS = 512
D = 1024
HALF = 64
CHUNKS = 6
SCALE = 20.0
LOG_SCALE = math.log(SCALE)
PARTS = 2
WIDTH = D // PARTS
MASKED = -1e30
F32 = jnp.float32
BF16 = jnp.bfloat16
BLOCKS = ROWS // BLK


def dot_rows(former, latter):
    return lax.dot_general(former, latter, (((1,), (1,)), ((), ())), preferred_element_type=F32)


def dot(former, latter):
    return jnp.dot(former, latter, preferred_element_type=F32)


def rows_of(b):
    return pl.ds(b * BLK, BLK)


def lanes(shape):
    return lax.broadcasted_iota(jnp.int32, shape, len(shape) - 1)


def eye():
    shape = (BLK, BLK)
    return lax.broadcasted_iota(jnp.int32, shape, 0) == lanes(shape)


def to_lanes(column):
    return jnp.sum(jnp.where(eye(), column, 0.0), axis=0, keepdims=True)


def wide(column):
    return jnp.broadcast_to(column[:, :1], (BLK, D))


def exchange(
    q_hbm, r_hbm, cluster_hbm,
    g1, g2, h1, e_own, r_own, scale_g1, factors, w_last, last_q, loss_q, loss_r,
    q_own, m_col, z_col, held, s_own, t_own, x_ref, msg_right, msg_left, got_left, got_right, ids,
    send_sem, recv_sem, msg_send, msg_recv, load_sem,
):
    shape_wide, shape_narrow = lax.axis_size("wide"), lax.axis_size("narrow")
    count = shape_wide * shape_narrow
    me = lax.axis_index("wide") * shape_narrow + lax.axis_index("narrow")
    left, right = lax.rem(me + count - 1, count), lax.rem(me + 1, count)

    def coords(p):
        return (lax.div(p, shape_narrow), lax.rem(p, shape_narrow))

    loads = [
        pltpu.make_async_copy(q_hbm, q_own, load_sem.at[0]),
        pltpu.make_async_copy(r_hbm, r_own, load_sem.at[1]),
        pltpu.make_async_copy(cluster_hbm, ids, load_sem.at[2]),
    ]
    has_left, has_right = me > 0, me < count - 1
    barrier = pltpu.get_barrier_semaphore()
    for p, exists in ((left, has_left), (right, has_right)):

        @pl.when(exists)
        def _():
            pl.semaphore_signal(barrier, inc=1, device_id=coords(p), device_id_type=MESH)

    for inner, signals in ((has_left & has_right, 2), (jnp.logical_not(has_left & has_right), 1)):

        @pl.when(inner)
        def _():
            pl.semaphore_wait(barrier, signals)

    def copies(src, slot, c):
        landing = last_q if isinstance(slot, int) and slot == 2 * CHUNKS - 1 else held.at[slot]
        to_right = pltpu.make_async_remote_copy(
            src_ref=src.at[pl.ds(BLK + c * HALF, HALF)],
            dst_ref=landing.at[pl.ds(0, HALF)],
            send_sem=send_sem.at[slot, 0],
            recv_sem=recv_sem.at[slot, 0],
            device_id=coords(right),
            device_id_type=MESH,
        )
        to_left = pltpu.make_async_remote_copy(
            src_ref=src.at[pl.ds(c * HALF, HALF)],
            dst_ref=landing.at[pl.ds(HALF, HALF)],
            send_sem=send_sem.at[slot, 1],
            recv_sem=recv_sem.at[slot, 1],
            device_id=coords(left),
            device_id_type=MESH,
        )
        return to_right, to_left

    def started(pair):
        to_right, to_left = pair
        pl.when(has_right)(to_right.start)
        pl.when(has_left)(to_left.start)

    def received(pair):
        from_left, from_right = pair
        pl.when(has_left)(from_left.wait_recv)
        pl.when(has_right)(from_right.wait_recv)

    def sent(pair):
        to_right, to_left = pair
        pl.when(has_right)(to_right.wait_send)
        pl.when(has_left)(to_left.wait_send)

    def start(src, slot, c):
        started(copies(src, slot, c))

    def landed(src, slot, c):
        received(copies(src, slot, c))

    start(r_hbm, 0, 0)
    for load in loads:
        load.start()
    for c in range(1, CHUNKS):
        start(r_hbm, c, c)

    for exists, at, got in ((has_left, 0, got_left), (has_right, HALF, got_right)):

        @pl.when(jnp.logical_not(exists))
        def _():
            held[:, pl.ds(at, HALF)] = jnp.zeros((2 * CHUNKS - 1, HALF, D), BF16)
            last_q[pl.ds(at, HALF)] = jnp.zeros((HALF, D), BF16)
            got[...] = jnp.zeros_like(got)

    for load in loads:
        load.wait()
    own_ids = [ids[me * BLOCKS + b] for b in range(BLOCKS)]
    lane = lanes((1, ROWS))
    id_row = jnp.full((1, ROWS), own_ids[0], jnp.int32)
    for b in range(1, BLOCKS):
        id_row = jnp.where(lane >= b * BLK, own_ids[b], id_row)

    for b in range(BLOCKS):
        allowed = jnp.broadcast_to(id_row == own_ids[b], (BLK, ROWS))
        s_own[rows_of(b)] = jnp.where(allowed, dot_rows(q_own[rows_of(b)], r_own[...]) * SCALE, MASKED)
        t_own[rows_of(b)] = jnp.where(allowed, dot_rows(r_own[rows_of(b)], q_own[...]) * SCALE, MASKED)

    def sums_by_lane(scores):
        largest = jnp.max(scores[...], axis=0, keepdims=True)
        return largest, jnp.sum(jnp.exp(scores[...] - largest), axis=0, keepdims=True)

    largest_cols, summed_cols = sums_by_lane(s_own)
    largest_rows, summed_rows = sums_by_lane(t_own)
    for k, lse in enumerate((largest_cols + jnp.log(summed_cols), largest_rows + jnp.log(summed_rows))):
        lse = jnp.broadcast_to(lse, (8, ROWS))
        ahead, behind = pltpu.roll(lse, ROWS - HALF, 1), pltpu.roll(lse, HALF, 1)
        for c in range(CHUNKS):
            at = (c // 2) * BLK
            row = pl.ds(8 * k + c, 1)
            msg_right[row] = (ahead if c % 2 else lse)[:1, BLK + at : 2 * BLK + at]
            msg_left[row] = (lse if c % 2 else behind)[:1, at : BLK + at]
        rest = pl.ds(8 * k + CHUNKS, 8 - CHUNKS)
        msg_right[rest] = jnp.zeros((8 - CHUNKS, BLK), F32)
        msg_left[rest] = jnp.zeros((8 - CHUNKS, BLK), F32)
    messages = [
        pltpu.make_async_remote_copy(
            src_ref=src,
            dst_ref=dst,
            send_sem=msg_send.at[k],
            recv_sem=msg_recv.at[k],
            device_id=coords(p),
            device_id_type=MESH,
        )
        for k, (src, dst, p) in enumerate(((msg_right, got_left, right), (msg_left, got_right, left)))
    ]
    started(messages)
    for c in range(CHUNKS):
        start(q_hbm, CHUNKS + c, c)

    for b in range(BLOCKS):
        rows = rows_of(b)
        x = t_own[rows]
        largest = jnp.max(x, axis=1, keepdims=True)
        e = jnp.exp(x - largest)
        m_col[rows] = jnp.broadcast_to(largest, (BLK, BLK))
        z_col[rows] = jnp.broadcast_to(jnp.sum(e, axis=1, keepdims=True), (BLK, BLK))
        g1[rows] = dot(e.astype(BF16), q_own[...])
    e_own[...] = jnp.exp(s_own[...] - largest_cols)

    first_half = lanes((1, BLK)) < HALF

    def ids_of(c):
        return jnp.where(first_half, ids[left * BLOCKS + 1 + c // 2], ids[right * BLOCKS + c // 2])

    def scores_of(c, chunk, own):
        id_chunk = ids_of(c)
        for b in range(BLOCKS):
            allowed = jnp.broadcast_to(id_chunk == own_ids[b], (BLK, BLK))
            x_ref[c, rows_of(b)] = jnp.where(allowed, dot_rows(own[rows_of(b)], chunk[...]) * SCALE, MASKED)

    def lse_of(c, msg_row):
        x = x_ref[c]
        msg = jnp.where(first_half, got_left[pl.ds(msg_row, 1)], got_right[pl.ds(msg_row, 1)])
        largest = jnp.maximum(jnp.max(x, axis=0, keepdims=True), msg)
        summed = jnp.exp(msg - largest) + jnp.sum(jnp.exp(x - largest), axis=0, keepdims=True)
        return largest + jnp.log(summed)

    def at_diagonal(b):
        shape = (BLK, ROWS)
        return lanes(shape) == lax.broadcasted_iota(jnp.int32, shape, 0) + b * BLK

    @pl.loop(0, CHUNKS)
    def _(c):
        landed(r_hbm, c, c)
        scores_of(c, held.at[c], q_own)

    received(messages)
    col_lse = jnp.concatenate([lse_of(c, c) for c in range(CHUNKS)], axis=1)
    row_lse, diagonals = [], []
    for b in range(BLOCKS):
        rows = rows_of(b)
        own = s_own[rows]
        others = jnp.concatenate([x_ref[c, rows] for c in range(CHUNKS)], axis=1)
        largest = jnp.maximum(jnp.max(own, axis=1, keepdims=True), jnp.max(others, axis=1, keepdims=True))
        summed = jnp.sum(jnp.exp(own - largest), axis=1, keepdims=True)
        summed += jnp.sum(jnp.exp(others - largest), axis=1, keepdims=True)
        lse = largest + jnp.log(summed)
        w_own = jnp.exp(own - lse) - jnp.where(at_diagonal(b), 1.0, 0.0)
        w_others = jnp.exp(others - lse) + jnp.exp(others - col_lse)
        h1[rows] = SCALE * (
            dot(w_own.astype(BF16), r_own[...])
            + dot(w_others.astype(BF16), held[:CHUNKS].reshape(CHUNKS * BLK, D))
        )
        row_lse.append(to_lanes(lse))
        diagonals.append(to_lanes(s_own[rows, b * BLK : (b + 1) * BLK]))
        loss_q[pl.ds(b, 1)] = row_lse[b] - diagonals[b]
    row_lse = jnp.concatenate(row_lse, axis=1)
    for b in range(BLOCKS):
        rows = rows_of(b)
        w = jnp.exp(t_own[rows] - row_lse) - jnp.where(at_diagonal(b), 1.0, 0.0)
        g2[rows] = SCALE * (dot(w.astype(BF16), q_own[...]) - q_own[rows].astype(F32))

    for first, end in ((0, CHUNKS // 2), (CHUNKS // 2, CHUNKS - 1)):

        @pl.loop(first, end)
        def _(c):
            landed(q_hbm, CHUNKS + c, c)
            scores_of(c, held.at[CHUNKS + c], r_own)

        group = range(first, end)
        lse = jnp.concatenate([lse_of(c, 8 + c) for c in group], axis=1)
        for b in range(BLOCKS):
            rows = rows_of(b)
            x = jnp.concatenate([x_ref[c, rows] for c in group], axis=1)
            before = m_col[rows]
            after = jnp.maximum(before, jnp.max(x, axis=1, keepdims=True))
            shrink = jnp.exp(before - after)
            e = jnp.exp(x - after[:, :1])
            m_col[rows] = after
            z_col[rows] = z_col[rows] * shrink + jnp.sum(e, axis=1, keepdims=True)
            queries = held[CHUNKS + first : CHUNKS + end].reshape(len(group) * BLK, D)
            g1[rows] = g1[rows] * wide(shrink) + dot(e.astype(BF16), queries)
            g2[rows] += dot(jnp.exp(x - (lse - LOG_SCALE)).astype(BF16), queries)

    c = CHUNKS - 1
    before = jnp.concatenate([to_lanes(m_col[rows_of(b)]) for b in range(BLOCKS)], axis=1)
    z_before = jnp.concatenate([to_lanes(z_col[rows_of(b)]) for b in range(BLOCKS)], axis=1)
    msg = jnp.where(first_half, got_left[pl.ds(8 + c, 1)], got_right[pl.ds(8 + c, 1)])
    msg = jnp.sum(jnp.where(eye(), msg, 0.0), axis=1, keepdims=True)
    shape = (BLK, ROWS)
    id_chunk = jnp.where(
        lax.broadcasted_iota(jnp.int32, shape, 0) < HALF, ids[left * BLOCKS + 1 + c // 2], ids[right * BLOCKS + c // 2]
    )
    allowed = id_chunk == jnp.broadcast_to(id_row, shape)
    landed(q_hbm, CHUNKS + c, c)
    x = jnp.where(allowed, dot_rows(last_q[...], r_own[...]) * SCALE, MASKED)
    after = jnp.maximum(before, jnp.max(x, axis=0, keepdims=True))
    shrink = jnp.exp(before - after)
    e = jnp.exp(x - after)
    z = z_before * shrink + jnp.sum(e, axis=0, keepdims=True)
    inverse = SCALE / z
    col_lse = after + jnp.log(z)
    scale_g1[...] = jnp.broadcast_to(shrink * inverse, (8, ROWS))
    factors[...] = jnp.broadcast_to(SCALE * jnp.exp(largest_cols - col_lse), (8, ROWS))
    for b in range(BLOCKS):
        loss_r[pl.ds(b, 1)] = col_lse[:, b * BLK : (b + 1) * BLK] - diagonals[b]
    largest = jnp.maximum(jnp.max(x, axis=1, keepdims=True), msg)
    summed = jnp.exp(msg - largest) + jnp.sum(jnp.exp(x - largest), axis=1, keepdims=True)
    w_last[...] = e * inverse + jnp.exp(x - (largest + jnp.log(summed) - LOG_SCALE))
    for c in range(CHUNKS):
        for src, slot in ((r_hbm, c), (q_hbm, CHUNKS + c)):
            sent(copies(src, slot, c))
    sent(messages)


def finish(
    g1, g2, h1, e_own, r_own, scale_g1, factors, w_last, last_q, loss_q, loss_r,
    loss_q_out, loss_r_out, q_out, r_out,
    gq, gr, sems,
):
    writes = [
        pltpu.make_async_copy(loss_q, loss_q_out, sems.at[0]),
        pltpu.make_async_copy(loss_r, loss_r_out, sems.at[1]),
    ]
    for write in writes:
        write.start()

    def put(k, held, out, cols):
        writes.append(pltpu.make_async_copy(held.at[:, cols], out.at[:, cols], sems.at[2 + k]))
        writes[-1].start()

    diagonal = jnp.where(eye(), SCALE, 0.0)
    w_own = []
    for b in range(BLOCKS):
        at = slice(b * BLK, (b + 1) * BLK)
        w = e_own[rows_of(b)] * factors[:1]
        w_own.append(jnp.concatenate([p for p in (w[:, : at.start], w[:, at] - diagonal, w[:, at.stop :]) if p.shape[1]], axis=1))
    w_own = jnp.concatenate(w_own, axis=0).astype(BF16)
    for k in range(PARTS):
        cols = pl.ds(k * WIDTH, WIDTH)
        gq[:, cols] = (h1[:, cols] + dot(w_own, r_own[:, cols])).astype(BF16)
        put(k, gq, q_out, cols)
    blocks = [slice(b * BLK, (b + 1) * BLK) for b in range(BLOCKS)]
    w_cols = jnp.concatenate([jnp.transpose(w_last[:, at]) for at in blocks], axis=0).astype(BF16)
    scale = [jnp.transpose(jnp.broadcast_to(scale_g1[:1, at], (BLK, BLK))) for at in blocks]
    scale = jnp.concatenate(scale, axis=0)[:, :1]
    for k in range(PARTS):
        cols = pl.ds(k * WIDTH, WIDTH)
        total = g1[:, cols] * scale + g2[:, cols] + dot(w_cols, last_q[:, cols])
        gr[:, cols] = total.astype(BF16)
        put(PARTS + k, gr, r_out, cols)
    for write in writes:
        write.wait()


def shards(queries, responses, block_cluster):
    queries, responses, block_cluster = (
        pltpu.with_memory_space_constraint(a, pltpu.HBM) for a in (queries, responses, block_cluster)
    )
    vmem = pl.BlockSpec(memory_space=pltpu.VMEM)
    hbm = pl.BlockSpec(memory_space=pltpu.HBM)
    passed = (
        ((ROWS, D), F32),
        ((ROWS, D), F32),
        ((ROWS, D), F32),
        ((ROWS, ROWS), F32),
        ((ROWS, D), BF16),
        ((8, ROWS), F32),
        ((8, ROWS), F32),
        ((BLK, ROWS), F32),
        ((BLK, D), BF16),
        ((BLOCKS, BLK), F32),
        ((BLOCKS, BLK), F32),
    )
    parts = pl.pallas_call(
        exchange,
        out_shape=[pltpu.VMEM(shape, dtype) for shape, dtype in passed],
        in_specs=[hbm] * 3,
        out_specs=[vmem] * len(passed),
        scratch_shapes=[
            pltpu.VMEM((ROWS, D), BF16),
            pltpu.VMEM((ROWS, BLK), F32),
            pltpu.VMEM((ROWS, BLK), F32),
            pltpu.VMEM((2 * CHUNKS - 1, BLK, D), BF16),
            pltpu.VMEM((ROWS, ROWS), F32),
            pltpu.VMEM((ROWS, ROWS), F32),
            pltpu.VMEM((CHUNKS, ROWS, BLK), F32),
            pltpu.VMEM((16, BLK), F32),
            pltpu.VMEM((16, BLK), F32),
            pltpu.VMEM((16, BLK), F32),
            pltpu.VMEM((16, BLK), F32),
            pltpu.SMEM(block_cluster.shape, jnp.int32),
            pltpu.SemaphoreType.DMA((2 * CHUNKS, 2)),
            pltpu.SemaphoreType.DMA((2 * CHUNKS, 2)),
            pltpu.SemaphoreType.DMA((2,)),
            pltpu.SemaphoreType.DMA((2,)),
            pltpu.SemaphoreType.DMA((3,)),
        ],
        compiler_params=pltpu.CompilerParams(
            collective_id=0, has_side_effects=True, vmem_limit_bytes=32 * 2**20
        ),
        name="exchange",
    )(queries, responses, block_cluster)
    query_loss, response_loss, query_grad, response_grad = pl.pallas_call(
        finish,
        out_shape=[
            jax.ShapeDtypeStruct((BLOCKS, BLK), F32),
            jax.ShapeDtypeStruct((BLOCKS, BLK), F32),
            jax.ShapeDtypeStruct((ROWS, D), BF16),
            jax.ShapeDtypeStruct((ROWS, D), BF16),
        ],
        in_specs=[vmem] * len(passed),
        out_specs=[hbm] * 4,
        scratch_shapes=[
            pltpu.VMEM((ROWS, D), BF16),
            pltpu.VMEM((ROWS, D), BF16),
            pltpu.SemaphoreType.DMA((2 + 2 * PARTS,)),
        ],
        compiler_params=pltpu.CompilerParams(vmem_limit_bytes=32 * 2**20),
        name="finish",
    )(*parts)
    return query_loss.reshape(ROWS), response_loss.reshape(ROWS), query_grad, response_grad


def solution(mesh):
    both = ("wide", "narrow")
    return jax.shard_map(
        shards,
        mesh=mesh,
        in_specs=(P(both, None), P(both, None), P()),
        out_specs=(P(both), P(both), P(both, None), P(both, None)),
        check_vma=False,
    )
```

```python
import math

import jax
import jax.numpy as jnp
from jax import lax
from jax.experimental import pallas as pl
from jax.experimental.pallas import tpu as pltpu
from jax.sharding import PartitionSpec as P

MESH = pl.DeviceIdType.MESH
BLK = 128
ROWS = 512
D = 1024
HALF = 64
CHUNKS = 6
SCALE = 20.0
LOG_SCALE = math.log(SCALE)
PARTS = 2
R_PARCELS = ((0, 2), (2, 2), (4, 2))
Q_PARCELS = ((0, 2), (2, 1), (3, 1), (4, 1))
PARCELS = len(R_PARCELS) + len(Q_PARCELS) + 2
EARLY = 768
WIDTH = D // PARTS
MASKED = -1e30
F32 = jnp.float32
BF16 = jnp.bfloat16
BLOCKS = ROWS // BLK


def dot_rows(former, latter):
    return lax.dot_general(former, latter, (((1,), (1,)), ((), ())), preferred_element_type=F32)


def dot(former, latter):
    return jnp.dot(former, latter, preferred_element_type=F32)


def rows_of(b):
    return pl.ds(b * BLK, BLK)


def lanes(shape):
    return lax.broadcasted_iota(jnp.int32, shape, len(shape) - 1)


def eye():
    shape = (BLK, BLK)
    return lax.broadcasted_iota(jnp.int32, shape, 0) == lanes(shape)


def to_lanes(column):
    return jnp.sum(jnp.where(eye(), column, 0.0), axis=0, keepdims=True)


def wide(column):
    return jnp.broadcast_to(column[:, :1], (BLK, D))


def exchange(
    q_hbm, r_hbm, q_parts, r_parts, cluster_hbm,
    g1, g2, h1, e_own, r_own, scale_g1, factors, w_last, last_q, loss_q, loss_r,
    q_own, m_col, z_col, held, s_own, t_own, x_ref, msg_right, msg_left, got_left, got_right, ids,
    send_sem, recv_sem, msg_send, msg_recv, load_sem,
):
    shape_wide, shape_narrow = lax.axis_size("wide"), lax.axis_size("narrow")
    count = shape_wide * shape_narrow
    me = lax.axis_index("wide") * shape_narrow + lax.axis_index("narrow")
    left, right = lax.rem(me + count - 1, count), lax.rem(me + 1, count)

    def coords(p):
        return (lax.div(p, shape_narrow), lax.rem(p, shape_narrow))

    loads = [
        pltpu.make_async_copy(q_hbm, q_own, load_sem.at[0]),
        pltpu.make_async_copy(r_hbm, r_own, load_sem.at[1]),
        pltpu.make_async_copy(cluster_hbm, ids, load_sem.at[2]),
    ]
    has_left, has_right = me > 0, me < count - 1
    barrier = pltpu.get_barrier_semaphore()
    for p, exists in ((left, has_left), (right, has_right)):

        @pl.when(exists)
        def _():
            pl.semaphore_signal(barrier, inc=1, device_id=coords(p), device_id_type=MESH)

    for inner, signals in ((has_left & has_right, 2), (jnp.logical_not(has_left & has_right), 1)):

        @pl.when(inner)
        def _():
            pl.semaphore_wait(barrier, signals)

    early, late = pl.ds(0, EARLY), pl.ds(EARLY, D - EARLY)
    last = CHUNKS - 1
    parcels = [(r_parts, first, n, held.at[pl.ds(first, n)], None) for first, n in R_PARCELS]
    parcels += [(q_parts, first, n, held.at[pl.ds(CHUNKS + first, n)], None) for first, n in Q_PARCELS]
    parcels += [(q_parts, last, 1, last_q, cols) for cols in (early, late)]

    def copies(k):
        src, first, n, dst, cols = parcels[k]
        pair = []
        for side, p in enumerate((right, left)):
            begin = first if side else first + BLK // HALF
            half = pl.ds(side * HALF, HALF)
            pair.append(
                pltpu.make_async_remote_copy(
                    src_ref=src.at[pl.ds(begin, n)] if cols is None else src.at[begin, :, cols],
                    dst_ref=dst.at[:, half] if cols is None else dst.at[half, cols],
                    send_sem=send_sem.at[k, side],
                    recv_sem=recv_sem.at[k, side],
                    device_id=coords(p),
                    device_id_type=MESH,
                )
            )
        return pair

    def started(pair):
        to_right, to_left = pair
        pl.when(has_right)(to_right.start)
        pl.when(has_left)(to_left.start)

    def received(pair):
        from_left, from_right = pair
        pl.when(has_left)(from_left.wait_recv)
        pl.when(has_right)(from_right.wait_recv)

    def sent(pair):
        to_right, to_left = pair
        pl.when(has_right)(to_right.wait_send)
        pl.when(has_left)(to_left.wait_send)

    for k in range(len(R_PARCELS)):
        started(copies(k))
    for load in loads:
        load.start()

    for exists, at, got in ((has_left, 0, got_left), (has_right, HALF, got_right)):

        @pl.when(jnp.logical_not(exists))
        def _():
            held[:, pl.ds(at, HALF)] = jnp.zeros((2 * CHUNKS - 1, HALF, D), BF16)
            last_q[pl.ds(at, HALF)] = jnp.zeros((HALF, D), BF16)
            got[...] = jnp.zeros_like(got)

    for load in loads:
        load.wait()
    own_ids = [ids[me * BLOCKS + b] for b in range(BLOCKS)]
    lane = lanes((1, ROWS))
    id_row = jnp.full((1, ROWS), own_ids[0], jnp.int32)
    for b in range(1, BLOCKS):
        id_row = jnp.where(lane >= b * BLK, own_ids[b], id_row)

    for b in range(BLOCKS):
        allowed = jnp.broadcast_to(id_row == own_ids[b], (BLK, ROWS))
        s_own[rows_of(b)] = jnp.where(allowed, dot_rows(q_own[rows_of(b)], r_own[...]) * SCALE, MASKED)
        t_own[rows_of(b)] = jnp.where(allowed, dot_rows(r_own[rows_of(b)], q_own[...]) * SCALE, MASKED)

    def sums_by_lane(scores):
        largest = jnp.max(scores[...], axis=0, keepdims=True)
        return largest, jnp.sum(jnp.exp(scores[...] - largest), axis=0, keepdims=True)

    largest_cols, summed_cols = sums_by_lane(s_own)
    largest_rows, summed_rows = sums_by_lane(t_own)
    for k, lse in enumerate((largest_cols + jnp.log(summed_cols), largest_rows + jnp.log(summed_rows))):
        lse = jnp.broadcast_to(lse, (8, ROWS))
        ahead, behind = pltpu.roll(lse, ROWS - HALF, 1), pltpu.roll(lse, HALF, 1)
        for c in range(CHUNKS):
            at = (c // 2) * BLK
            row = pl.ds(8 * k + c, 1)
            msg_right[row] = (ahead if c % 2 else lse)[:1, BLK + at : 2 * BLK + at]
            msg_left[row] = (lse if c % 2 else behind)[:1, at : BLK + at]
        rest = pl.ds(8 * k + CHUNKS, 8 - CHUNKS)
        msg_right[rest] = jnp.zeros((8 - CHUNKS, BLK), F32)
        msg_left[rest] = jnp.zeros((8 - CHUNKS, BLK), F32)
    messages = [
        pltpu.make_async_remote_copy(
            src_ref=src,
            dst_ref=dst,
            send_sem=msg_send.at[k],
            recv_sem=msg_recv.at[k],
            device_id=coords(p),
            device_id_type=MESH,
        )
        for k, (src, dst, p) in enumerate(((msg_right, got_left, right), (msg_left, got_right, left)))
    ]
    started(messages)
    for k in range(len(R_PARCELS), len(parcels)):
        started(copies(k))

    for b in range(BLOCKS):
        rows = rows_of(b)
        x = t_own[rows]
        largest = jnp.max(x, axis=1, keepdims=True)
        e = jnp.exp(x - largest)
        m_col[rows] = jnp.broadcast_to(largest, (BLK, BLK))
        z_col[rows] = jnp.broadcast_to(jnp.sum(e, axis=1, keepdims=True), (BLK, BLK))
        g1[rows] = dot(e.astype(BF16), q_own[...])
    e_own[...] = jnp.exp(s_own[...] - largest_cols)

    first_half = lanes((1, BLK)) < HALF

    def ids_of(c):
        return jnp.where(first_half, ids[left * BLOCKS + 1 + c // 2], ids[right * BLOCKS + c // 2])

    def scores_of(c, chunk, own):
        id_chunk = ids_of(c)
        for b in range(BLOCKS):
            allowed = jnp.broadcast_to(id_chunk == own_ids[b], (BLK, BLK))
            x_ref[c, rows_of(b)] = jnp.where(allowed, dot_rows(own[rows_of(b)], chunk[...]) * SCALE, MASKED)

    def lse_of(c, msg_row):
        x = x_ref[c]
        msg = jnp.where(first_half, got_left[pl.ds(msg_row, 1)], got_right[pl.ds(msg_row, 1)])
        largest = jnp.maximum(jnp.max(x, axis=0, keepdims=True), msg)
        summed = jnp.exp(msg - largest) + jnp.sum(jnp.exp(x - largest), axis=0, keepdims=True)
        return largest + jnp.log(summed)

    def at_diagonal(b):
        shape = (BLK, ROWS)
        return lanes(shape) == lax.broadcasted_iota(jnp.int32, shape, 0) + b * BLK

    for k, (first, n) in enumerate(R_PARCELS):
        received(copies(k))
        for c in range(first, first + n):
            scores_of(c, held.at[c], q_own)

    received(messages)
    col_lse = jnp.concatenate([lse_of(c, c) for c in range(CHUNKS)], axis=1)
    row_lse, diagonals = [], []
    for b in range(BLOCKS):
        rows = rows_of(b)
        own = s_own[rows]
        others = jnp.concatenate([x_ref[c, rows] for c in range(CHUNKS)], axis=1)
        largest = jnp.maximum(jnp.max(own, axis=1, keepdims=True), jnp.max(others, axis=1, keepdims=True))
        summed = jnp.sum(jnp.exp(own - largest), axis=1, keepdims=True)
        summed += jnp.sum(jnp.exp(others - largest), axis=1, keepdims=True)
        lse = largest + jnp.log(summed)
        w_own = jnp.exp(own - lse) - jnp.where(at_diagonal(b), 1.0, 0.0)
        w_others = jnp.exp(others - lse) + jnp.exp(others - col_lse)
        h1[rows] = SCALE * (
            dot(w_own.astype(BF16), r_own[...])
            + dot(w_others.astype(BF16), held[:CHUNKS].reshape(CHUNKS * BLK, D))
        )
        row_lse.append(to_lanes(lse))
        diagonals.append(to_lanes(s_own[rows, b * BLK : (b + 1) * BLK]))
        loss_q[pl.ds(b, 1)] = row_lse[b] - diagonals[b]
    row_lse = jnp.concatenate(row_lse, axis=1)
    for b in range(BLOCKS):
        rows = rows_of(b)
        w = jnp.exp(t_own[rows] - row_lse) - jnp.where(at_diagonal(b), 1.0, 0.0)
        g2[rows] = SCALE * (dot(w.astype(BF16), q_own[...]) - q_own[rows].astype(F32))

    for first, end in ((0, CHUNKS // 2), (CHUNKS // 2, CHUNKS - 1)):

        for k, (src, begin, n, _, cols) in enumerate(parcels):
            if src is q_parts and cols is None and first <= begin < end:
                received(copies(k))
                for c in range(begin, begin + n):
                    scores_of(c, held.at[CHUNKS + c], r_own)

        group = range(first, end)
        lse = jnp.concatenate([lse_of(c, 8 + c) for c in group], axis=1)
        for b in range(BLOCKS):
            rows = rows_of(b)
            x = jnp.concatenate([x_ref[c, rows] for c in group], axis=1)
            before = m_col[rows]
            after = jnp.maximum(before, jnp.max(x, axis=1, keepdims=True))
            shrink = jnp.exp(before - after)
            e = jnp.exp(x - after[:, :1])
            m_col[rows] = after
            z_col[rows] = z_col[rows] * shrink + jnp.sum(e, axis=1, keepdims=True)
            queries = held[CHUNKS + first : CHUNKS + end].reshape(len(group) * BLK, D)
            g1[rows] = g1[rows] * wide(shrink) + dot(e.astype(BF16), queries)
            g2[rows] += dot(jnp.exp(x - (lse - LOG_SCALE)).astype(BF16), queries)

    c = CHUNKS - 1
    before = jnp.concatenate([to_lanes(m_col[rows_of(b)]) for b in range(BLOCKS)], axis=1)
    z_before = jnp.concatenate([to_lanes(z_col[rows_of(b)]) for b in range(BLOCKS)], axis=1)
    msg = jnp.where(first_half, got_left[pl.ds(8 + c, 1)], got_right[pl.ds(8 + c, 1)])
    msg = jnp.sum(jnp.where(eye(), msg, 0.0), axis=1, keepdims=True)
    shape = (BLK, ROWS)
    id_chunk = jnp.where(
        lax.broadcasted_iota(jnp.int32, shape, 0) < HALF, ids[left * BLOCKS + 1 + c // 2], ids[right * BLOCKS + c // 2]
    )
    allowed = id_chunk == jnp.broadcast_to(id_row, shape)
    received(copies(len(parcels) - 2))
    x = dot_rows(last_q[:, early], r_own[:, early])
    received(copies(len(parcels) - 1))
    x += dot_rows(last_q[:, late], r_own[:, late])
    x = jnp.where(allowed, x * SCALE, MASKED)
    after = jnp.maximum(before, jnp.max(x, axis=0, keepdims=True))
    shrink = jnp.exp(before - after)
    e = jnp.exp(x - after)
    z = z_before * shrink + jnp.sum(e, axis=0, keepdims=True)
    inverse = SCALE / z
    col_lse = after + jnp.log(z)
    scale_g1[...] = jnp.broadcast_to(shrink * inverse, (8, ROWS))
    factors[...] = jnp.broadcast_to(SCALE * jnp.exp(largest_cols - col_lse), (8, ROWS))
    for b in range(BLOCKS):
        loss_r[pl.ds(b, 1)] = col_lse[:, b * BLK : (b + 1) * BLK] - diagonals[b]
    largest = jnp.maximum(jnp.max(x, axis=1, keepdims=True), msg)
    summed = jnp.exp(msg - largest) + jnp.sum(jnp.exp(x - largest), axis=1, keepdims=True)
    w_last[...] = e * inverse + jnp.exp(x - (largest + jnp.log(summed) - LOG_SCALE))
    for k in range(len(parcels)):
        sent(copies(k))
    sent(messages)


def finish(
    g1, g2, h1, e_own, r_own, scale_g1, factors, w_last, last_q, loss_q, loss_r,
    loss_q_out, loss_r_out, q_out, r_out,
    gq, gr, sems,
):
    writes = [
        pltpu.make_async_copy(loss_q, loss_q_out, sems.at[0]),
        pltpu.make_async_copy(loss_r, loss_r_out, sems.at[1]),
    ]
    for write in writes:
        write.start()

    def put(k, held, out, cols):
        writes.append(pltpu.make_async_copy(held.at[:, cols], out.at[:, cols], sems.at[2 + k]))
        writes[-1].start()

    diagonal = jnp.where(eye(), SCALE, 0.0)
    w_own = []
    for b in range(BLOCKS):
        at = slice(b * BLK, (b + 1) * BLK)
        w = e_own[rows_of(b)] * factors[:1]
        w_own.append(jnp.concatenate([p for p in (w[:, : at.start], w[:, at] - diagonal, w[:, at.stop :]) if p.shape[1]], axis=1))
    w_own = jnp.concatenate(w_own, axis=0).astype(BF16)
    for k in range(PARTS):
        cols = pl.ds(k * WIDTH, WIDTH)
        gq[:, cols] = (h1[:, cols] + dot(w_own, r_own[:, cols])).astype(BF16)
        put(k, gq, q_out, cols)
    blocks = [slice(b * BLK, (b + 1) * BLK) for b in range(BLOCKS)]
    w_cols = jnp.concatenate([jnp.transpose(w_last[:, at]) for at in blocks], axis=0).astype(BF16)
    scale = [jnp.transpose(jnp.broadcast_to(scale_g1[:1, at], (BLK, BLK))) for at in blocks]
    scale = jnp.concatenate(scale, axis=0)[:, :1]
    for k in range(PARTS):
        cols = pl.ds(k * WIDTH, WIDTH)
        total = g1[:, cols] * scale + g2[:, cols] + dot(w_cols, last_q[:, cols])
        gr[:, cols] = total.astype(BF16)
        put(PARTS + k, gr, r_out, cols)
    for write in writes:
        write.wait()


def shards(queries, responses, block_cluster):
    parts = [
        pltpu.with_memory_space_constraint(a.reshape(ROWS // HALF, HALF, D), pltpu.HBM) for a in (queries, responses)
    ]
    queries, responses, block_cluster = (
        pltpu.with_memory_space_constraint(a, pltpu.HBM) for a in (queries, responses, block_cluster)
    )
    vmem = pl.BlockSpec(memory_space=pltpu.VMEM)
    hbm = pl.BlockSpec(memory_space=pltpu.HBM)
    passed = (
        ((ROWS, D), F32),
        ((ROWS, D), F32),
        ((ROWS, D), F32),
        ((ROWS, ROWS), F32),
        ((ROWS, D), BF16),
        ((8, ROWS), F32),
        ((8, ROWS), F32),
        ((BLK, ROWS), F32),
        ((BLK, D), BF16),
        ((BLOCKS, BLK), F32),
        ((BLOCKS, BLK), F32),
    )
    sums = pl.pallas_call(
        exchange,
        out_shape=[pltpu.VMEM(shape, dtype) for shape, dtype in passed],
        in_specs=[hbm] * 5,
        out_specs=[vmem] * len(passed),
        scratch_shapes=[
            pltpu.VMEM((ROWS, D), BF16),
            pltpu.VMEM((ROWS, BLK), F32),
            pltpu.VMEM((ROWS, BLK), F32),
            pltpu.VMEM((2 * CHUNKS - 1, BLK, D), BF16),
            pltpu.VMEM((ROWS, ROWS), F32),
            pltpu.VMEM((ROWS, ROWS), F32),
            pltpu.VMEM((CHUNKS, ROWS, BLK), F32),
            pltpu.VMEM((16, BLK), F32),
            pltpu.VMEM((16, BLK), F32),
            pltpu.VMEM((16, BLK), F32),
            pltpu.VMEM((16, BLK), F32),
            pltpu.SMEM(block_cluster.shape, jnp.int32),
            pltpu.SemaphoreType.DMA((PARCELS, 2)),
            pltpu.SemaphoreType.DMA((PARCELS, 2)),
            pltpu.SemaphoreType.DMA((2,)),
            pltpu.SemaphoreType.DMA((2,)),
            pltpu.SemaphoreType.DMA((3,)),
        ],
        compiler_params=pltpu.CompilerParams(
            collective_id=0, has_side_effects=True, vmem_limit_bytes=32 * 2**20
        ),
        name="exchange",
    )(queries, responses, *parts, block_cluster)
    query_loss, response_loss, query_grad, response_grad = pl.pallas_call(
        finish,
        out_shape=[
            jax.ShapeDtypeStruct((BLOCKS, BLK), F32),
            jax.ShapeDtypeStruct((BLOCKS, BLK), F32),
            jax.ShapeDtypeStruct((ROWS, D), BF16),
            jax.ShapeDtypeStruct((ROWS, D), BF16),
        ],
        in_specs=[vmem] * len(passed),
        out_specs=[hbm] * 4,
        scratch_shapes=[
            pltpu.VMEM((ROWS, D), BF16),
            pltpu.VMEM((ROWS, D), BF16),
            pltpu.SemaphoreType.DMA((2 + 2 * PARTS,)),
        ],
        compiler_params=pltpu.CompilerParams(vmem_limit_bytes=32 * 2**20),
        name="finish",
    )(*sums)
    return query_loss.reshape(ROWS), response_loss.reshape(ROWS), query_grad, response_grad


def solution(mesh):
    both = ("wide", "narrow")
    return jax.shard_map(
        shards,
        mesh=mesh,
        in_specs=(P(both, None), P(both, None), P()),
        out_specs=(P(both), P(both), P(both, None), P(both, None)),
        check_vma=False,
    )
```

```python
import math

import jax
import jax.numpy as jnp
from jax import lax
from jax.experimental import pallas as pl
from jax.experimental.pallas import tpu as pltpu
from jax.sharding import PartitionSpec as P

MESH = pl.DeviceIdType.MESH
BLK = 128
ROWS = 512
D = 1024
HALF = 64
CHUNKS = 6
SCALE = 20.0
LOG_SCALE = math.log(SCALE)
PARTS = 2
WIDTH = D // PARTS
MASKED = -1e30
F32 = jnp.float32
BF16 = jnp.bfloat16
BLOCKS = ROWS // BLK


def dot_rows(former, latter):
    return lax.dot_general(former, latter, (((1,), (1,)), ((), ())), preferred_element_type=F32)


def dot(former, latter):
    return jnp.dot(former, latter, preferred_element_type=F32)


def rows_of(b):
    return pl.ds(b * BLK, BLK)


def lanes(shape):
    return lax.broadcasted_iota(jnp.int32, shape, len(shape) - 1)


def eye():
    shape = (BLK, BLK)
    return lax.broadcasted_iota(jnp.int32, shape, 0) == lanes(shape)


def to_lanes(column):
    return jnp.sum(jnp.where(eye(), column, 0.0), axis=0, keepdims=True)


def wide(column):
    return jnp.broadcast_to(column[:, :1], (BLK, D))


def exchange(
    q_hbm, r_hbm, cluster_hbm,
    g1, g2, h1, e_own, r_own, scale_g1, factors, w_last, last_q, loss_q, loss_r,
    q_own, m_col, z_col, held, s_own, t_own, x_ref, msg_right, msg_left, got_left, got_right, ids,
    send_sem, recv_sem, msg_send, msg_recv, load_sem,
):
    shape_wide, shape_narrow = lax.axis_size("wide"), lax.axis_size("narrow")
    count = shape_wide * shape_narrow
    me = lax.axis_index("wide") * shape_narrow + lax.axis_index("narrow")
    left, right = lax.rem(me + count - 1, count), lax.rem(me + 1, count)

    def coords(p):
        return (lax.div(p, shape_narrow), lax.rem(p, shape_narrow))

    loads = [
        pltpu.make_async_copy(q_hbm, q_own, load_sem.at[0]),
        pltpu.make_async_copy(r_hbm, r_own, load_sem.at[1]),
        pltpu.make_async_copy(cluster_hbm, ids, load_sem.at[2]),
    ]
    has_left, has_right = me > 0, me < count - 1
    barrier = pltpu.get_barrier_semaphore()
    for p, exists in ((left, has_left), (right, has_right)):

        @pl.when(exists)
        def _():
            pl.semaphore_signal(barrier, inc=1, device_id=coords(p), device_id_type=MESH)

    for inner, signals in ((has_left & has_right, 2), (jnp.logical_not(has_left & has_right), 1)):

        @pl.when(inner)
        def _():
            pl.semaphore_wait(barrier, signals)

    def copies(src, slot, c):
        landing = last_q if isinstance(slot, int) and slot == 2 * CHUNKS - 1 else held.at[slot]
        to_right = pltpu.make_async_remote_copy(
            src_ref=src.at[pl.ds(BLK + c * HALF, HALF)],
            dst_ref=landing.at[pl.ds(0, HALF)],
            send_sem=send_sem.at[slot, 0],
            recv_sem=recv_sem.at[slot, 0],
            device_id=coords(right),
            device_id_type=MESH,
        )
        to_left = pltpu.make_async_remote_copy(
            src_ref=src.at[pl.ds(c * HALF, HALF)],
            dst_ref=landing.at[pl.ds(HALF, HALF)],
            send_sem=send_sem.at[slot, 1],
            recv_sem=recv_sem.at[slot, 1],
            device_id=coords(left),
            device_id_type=MESH,
        )
        return to_right, to_left

    def started(pair):
        to_right, to_left = pair
        pl.when(has_right)(to_right.start)
        pl.when(has_left)(to_left.start)

    def received(pair):
        from_left, from_right = pair
        pl.when(has_left)(from_left.wait_recv)
        pl.when(has_right)(from_right.wait_recv)

    def sent(pair):
        to_right, to_left = pair
        pl.when(has_right)(to_right.wait_send)
        pl.when(has_left)(to_left.wait_send)

    def start(src, slot, c):
        started(copies(src, slot, c))

    def landed(src, slot, c):
        received(copies(src, slot, c))

    start(r_hbm, 0, 0)
    for load in loads:
        load.start()
    for c in range(1, CHUNKS):
        start(r_hbm, c, c)

    for exists, at, got in ((has_left, 0, got_left), (has_right, HALF, got_right)):

        @pl.when(jnp.logical_not(exists))
        def _():
            held[:, pl.ds(at, HALF)] = jnp.zeros((2 * CHUNKS - 1, HALF, D), BF16)
            last_q[pl.ds(at, HALF)] = jnp.zeros((HALF, D), BF16)
            got[...] = jnp.zeros_like(got)

    for load in loads:
        load.wait()
    own_ids = [ids[me * BLOCKS + b] for b in range(BLOCKS)]
    lane = lanes((1, ROWS))
    id_row = jnp.full((1, ROWS), own_ids[0], jnp.int32)
    for b in range(1, BLOCKS):
        id_row = jnp.where(lane >= b * BLK, own_ids[b], id_row)

    for b in range(BLOCKS):
        allowed = jnp.broadcast_to(id_row == own_ids[b], (BLK, ROWS))
        s_own[rows_of(b)] = jnp.where(allowed, dot_rows(q_own[rows_of(b)], r_own[...]) * SCALE, MASKED)
        t_own[rows_of(b)] = jnp.where(allowed, dot_rows(r_own[rows_of(b)], q_own[...]) * SCALE, MASKED)

    def sums_by_lane(scores):
        largest = jnp.max(scores[...], axis=0, keepdims=True)
        return largest, jnp.sum(jnp.exp(scores[...] - largest), axis=0, keepdims=True)

    largest_cols, summed_cols = sums_by_lane(s_own)
    largest_rows, summed_rows = sums_by_lane(t_own)
    first_half = lanes((1, BLK)) < HALF
    of_cols, of_rows = largest_cols + jnp.log(summed_cols), largest_rows + jnp.log(summed_rows)

    def shifted(lse, by):
        return pltpu.roll(jnp.broadcast_to(lse, (8, ROWS)), by, 1)[:1]

    ahead = [shifted(lse, ROWS - HALF) for lse in (of_cols, of_rows)]
    behind = [shifted(lse, HALF) for lse in (of_cols, of_rows)]
    for c in range(CHUNKS):
        here = slice((c // 2) * BLK, (c // 2 + 1) * BLK)
        after = slice(here.start + BLK, here.stop + BLK)
        row = pl.ds(c, 1)
        if c % 2:
            msg_right[row] = jnp.where(first_half, ahead[0][:, after], of_rows[:, after])
            msg_left[row] = jnp.where(first_half, ahead[1][:, here], of_cols[:, here])
        else:
            msg_right[row] = jnp.where(first_half, of_cols[:, after], behind[1][:, after])
            msg_left[row] = jnp.where(first_half, of_rows[:, here], behind[0][:, here])
    rest = pl.ds(CHUNKS, 8 - CHUNKS)
    for msg in (msg_right, msg_left):
        msg[rest] = jnp.zeros((8 - CHUNKS, BLK), F32)
    messages = [
        pltpu.make_async_remote_copy(
            src_ref=src,
            dst_ref=dst,
            send_sem=msg_send.at[k],
            recv_sem=msg_recv.at[k],
            device_id=coords(p),
            device_id_type=MESH,
        )
        for k, (src, dst, p) in enumerate(((msg_right, got_left, right), (msg_left, got_right, left)))
    ]
    started(messages)
    for c in range(CHUNKS):
        start(q_hbm, CHUNKS + c, c)

    for b in range(BLOCKS):
        rows = rows_of(b)
        x = t_own[rows]
        largest = jnp.max(x, axis=1, keepdims=True)
        e = jnp.exp(x - largest)
        m_col[rows] = jnp.broadcast_to(largest, (BLK, BLK))
        z_col[rows] = jnp.broadcast_to(jnp.sum(e, axis=1, keepdims=True), (BLK, BLK))
        g1[rows] = dot(e.astype(BF16), q_own[...])
    e_own[...] = jnp.exp(s_own[...] - largest_cols)

    def cols_message(c):
        return jnp.where(first_half, got_left[pl.ds(c, 1)], got_right[pl.ds(c, 1)])

    def rows_message(c):
        swapped = jnp.where(first_half, got_right[pl.ds(c, 1)], got_left[pl.ds(c, 1)])
        return pltpu.roll(jnp.broadcast_to(swapped, (8, BLK)), HALF, 1)[:1]

    def ids_of(c):
        return jnp.where(first_half, ids[left * BLOCKS + 1 + c // 2], ids[right * BLOCKS + c // 2])

    def scores_of(c, chunk, own):
        id_chunk = ids_of(c)
        for b in range(BLOCKS):
            allowed = jnp.broadcast_to(id_chunk == own_ids[b], (BLK, BLK))
            x_ref[c, rows_of(b)] = jnp.where(allowed, dot_rows(own[rows_of(b)], chunk[...]) * SCALE, MASKED)

    def lse_of(c, msg):
        x = x_ref[c]
        largest = jnp.maximum(jnp.max(x, axis=0, keepdims=True), msg)
        summed = jnp.exp(msg - largest) + jnp.sum(jnp.exp(x - largest), axis=0, keepdims=True)
        return largest + jnp.log(summed)

    def at_diagonal(b):
        shape = (BLK, ROWS)
        return lanes(shape) == lax.broadcasted_iota(jnp.int32, shape, 0) + b * BLK

    @pl.loop(0, CHUNKS)
    def _(c):
        landed(r_hbm, c, c)
        scores_of(c, held.at[c], q_own)

    received(messages)
    col_lse = jnp.concatenate([lse_of(c, cols_message(c)) for c in range(CHUNKS)], axis=1)
    row_lse, diagonals = [], []
    for b in range(BLOCKS):
        rows = rows_of(b)
        own = s_own[rows]
        others = jnp.concatenate([x_ref[c, rows] for c in range(CHUNKS)], axis=1)
        largest = jnp.maximum(jnp.max(own, axis=1, keepdims=True), jnp.max(others, axis=1, keepdims=True))
        summed = jnp.sum(jnp.exp(own - largest), axis=1, keepdims=True)
        summed += jnp.sum(jnp.exp(others - largest), axis=1, keepdims=True)
        lse = largest + jnp.log(summed)
        w_own = jnp.exp(own - lse) - jnp.where(at_diagonal(b), 1.0, 0.0)
        w_others = jnp.exp(others - lse) + jnp.exp(others - col_lse)
        h1[rows] = SCALE * (
            dot(w_own.astype(BF16), r_own[...])
            + dot(w_others.astype(BF16), held[:CHUNKS].reshape(CHUNKS * BLK, D))
        )
        row_lse.append(to_lanes(lse))
        diagonals.append(to_lanes(s_own[rows, b * BLK : (b + 1) * BLK]))
        loss_q[pl.ds(b, 1)] = row_lse[b] - diagonals[b]
    row_lse = jnp.concatenate(row_lse, axis=1)
    for b in range(BLOCKS):
        rows = rows_of(b)
        w = jnp.exp(t_own[rows] - row_lse) - jnp.where(at_diagonal(b), 1.0, 0.0)
        g2[rows] = SCALE * (dot(w.astype(BF16), q_own[...]) - q_own[rows].astype(F32))

    for first, end in ((0, CHUNKS // 2), (CHUNKS // 2, CHUNKS - 1)):

        @pl.loop(first, end)
        def _(c):
            landed(q_hbm, CHUNKS + c, c)
            scores_of(c, held.at[CHUNKS + c], r_own)

        group = range(first, end)
        lse = jnp.concatenate([lse_of(c, rows_message(c)) for c in group], axis=1)
        for b in range(BLOCKS):
            rows = rows_of(b)
            x = jnp.concatenate([x_ref[c, rows] for c in group], axis=1)
            before = m_col[rows]
            after = jnp.maximum(before, jnp.max(x, axis=1, keepdims=True))
            shrink = jnp.exp(before - after)
            e = jnp.exp(x - after[:, :1])
            m_col[rows] = after
            z_col[rows] = z_col[rows] * shrink + jnp.sum(e, axis=1, keepdims=True)
            queries = held[CHUNKS + first : CHUNKS + end].reshape(len(group) * BLK, D)
            g1[rows] = g1[rows] * wide(shrink) + dot(e.astype(BF16), queries)
            g2[rows] += dot(jnp.exp(x - (lse - LOG_SCALE)).astype(BF16), queries)

    c = CHUNKS - 1
    before = jnp.concatenate([to_lanes(m_col[rows_of(b)]) for b in range(BLOCKS)], axis=1)
    z_before = jnp.concatenate([to_lanes(z_col[rows_of(b)]) for b in range(BLOCKS)], axis=1)
    msg = rows_message(c)
    msg = jnp.sum(jnp.where(eye(), msg, 0.0), axis=1, keepdims=True)
    shape = (BLK, ROWS)
    id_chunk = jnp.where(
        lax.broadcasted_iota(jnp.int32, shape, 0) < HALF, ids[left * BLOCKS + 1 + c // 2], ids[right * BLOCKS + c // 2]
    )
    allowed = id_chunk == jnp.broadcast_to(id_row, shape)
    landed(q_hbm, CHUNKS + c, c)
    x = jnp.where(allowed, dot_rows(last_q[...], r_own[...]) * SCALE, MASKED)
    after = jnp.maximum(before, jnp.max(x, axis=0, keepdims=True))
    shrink = jnp.exp(before - after)
    e = jnp.exp(x - after)
    z = z_before * shrink + jnp.sum(e, axis=0, keepdims=True)
    inverse = SCALE / z
    col_lse = after + jnp.log(z)
    scale_g1[...] = jnp.broadcast_to(shrink * inverse, (8, ROWS))
    factors[...] = jnp.broadcast_to(SCALE * jnp.exp(largest_cols - col_lse), (8, ROWS))
    for b in range(BLOCKS):
        loss_r[pl.ds(b, 1)] = col_lse[:, b * BLK : (b + 1) * BLK] - diagonals[b]
    largest = jnp.maximum(jnp.max(x, axis=1, keepdims=True), msg)
    summed = jnp.exp(msg - largest) + jnp.sum(jnp.exp(x - largest), axis=1, keepdims=True)
    w_last[...] = e * inverse + jnp.exp(x - (largest + jnp.log(summed) - LOG_SCALE))
    for c in range(CHUNKS):
        for src, slot in ((r_hbm, c), (q_hbm, CHUNKS + c)):
            sent(copies(src, slot, c))
    sent(messages)


def finish(
    g1, g2, h1, e_own, r_own, scale_g1, factors, w_last, last_q, loss_q, loss_r,
    loss_q_out, loss_r_out, q_out, r_out,
    gq, gr, sems,
):
    writes = [
        pltpu.make_async_copy(loss_q, loss_q_out, sems.at[0]),
        pltpu.make_async_copy(loss_r, loss_r_out, sems.at[1]),
    ]
    for write in writes:
        write.start()

    def put(k, held, out, cols):
        writes.append(pltpu.make_async_copy(held.at[:, cols], out.at[:, cols], sems.at[2 + k]))
        writes[-1].start()

    diagonal = jnp.where(eye(), SCALE, 0.0)
    w_own = []
    for b in range(BLOCKS):
        at = slice(b * BLK, (b + 1) * BLK)
        w = e_own[rows_of(b)] * factors[:1]
        w_own.append(jnp.concatenate([p for p in (w[:, : at.start], w[:, at] - diagonal, w[:, at.stop :]) if p.shape[1]], axis=1))
    w_own = jnp.concatenate(w_own, axis=0).astype(BF16)
    for k in range(PARTS):
        cols = pl.ds(k * WIDTH, WIDTH)
        gq[:, cols] = (h1[:, cols] + dot(w_own, r_own[:, cols])).astype(BF16)
        put(k, gq, q_out, cols)
    blocks = [slice(b * BLK, (b + 1) * BLK) for b in range(BLOCKS)]
    w_cols = jnp.concatenate([jnp.transpose(w_last[:, at]) for at in blocks], axis=0).astype(BF16)
    scale = [jnp.transpose(jnp.broadcast_to(scale_g1[:1, at], (BLK, BLK))) for at in blocks]
    scale = jnp.concatenate(scale, axis=0)[:, :1]
    for k in range(PARTS):
        cols = pl.ds(k * WIDTH, WIDTH)
        total = g1[:, cols] * scale + g2[:, cols] + dot(w_cols, last_q[:, cols])
        gr[:, cols] = total.astype(BF16)
        put(PARTS + k, gr, r_out, cols)
    for write in writes:
        write.wait()


def shards(queries, responses, block_cluster):
    queries, responses, block_cluster = (
        pltpu.with_memory_space_constraint(a, pltpu.HBM) for a in (queries, responses, block_cluster)
    )
    vmem = pl.BlockSpec(memory_space=pltpu.VMEM)
    hbm = pl.BlockSpec(memory_space=pltpu.HBM)
    passed = (
        ((ROWS, D), F32),
        ((ROWS, D), F32),
        ((ROWS, D), F32),
        ((ROWS, ROWS), F32),
        ((ROWS, D), BF16),
        ((8, ROWS), F32),
        ((8, ROWS), F32),
        ((BLK, ROWS), F32),
        ((BLK, D), BF16),
        ((BLOCKS, BLK), F32),
        ((BLOCKS, BLK), F32),
    )
    parts = pl.pallas_call(
        exchange,
        out_shape=[pltpu.VMEM(shape, dtype) for shape, dtype in passed],
        in_specs=[hbm] * 3,
        out_specs=[vmem] * len(passed),
        scratch_shapes=[
            pltpu.VMEM((ROWS, D), BF16),
            pltpu.VMEM((ROWS, BLK), F32),
            pltpu.VMEM((ROWS, BLK), F32),
            pltpu.VMEM((2 * CHUNKS - 1, BLK, D), BF16),
            pltpu.VMEM((ROWS, ROWS), F32),
            pltpu.VMEM((ROWS, ROWS), F32),
            pltpu.VMEM((CHUNKS, ROWS, BLK), F32),
            pltpu.VMEM((8, BLK), F32),
            pltpu.VMEM((8, BLK), F32),
            pltpu.VMEM((8, BLK), F32),
            pltpu.VMEM((8, BLK), F32),
            pltpu.SMEM(block_cluster.shape, jnp.int32),
            pltpu.SemaphoreType.DMA((2 * CHUNKS, 2)),
            pltpu.SemaphoreType.DMA((2 * CHUNKS, 2)),
            pltpu.SemaphoreType.DMA((2,)),
            pltpu.SemaphoreType.DMA((2,)),
            pltpu.SemaphoreType.DMA((3,)),
        ],
        compiler_params=pltpu.CompilerParams(
            collective_id=0, has_side_effects=True, vmem_limit_bytes=32 * 2**20
        ),
        name="exchange",
    )(queries, responses, block_cluster)
    query_loss, response_loss, query_grad, response_grad = pl.pallas_call(
        finish,
        out_shape=[
            jax.ShapeDtypeStruct((BLOCKS, BLK), F32),
            jax.ShapeDtypeStruct((BLOCKS, BLK), F32),
            jax.ShapeDtypeStruct((ROWS, D), BF16),
            jax.ShapeDtypeStruct((ROWS, D), BF16),
        ],
        in_specs=[vmem] * len(passed),
        out_specs=[hbm] * 4,
        scratch_shapes=[
            pltpu.VMEM((ROWS, D), BF16),
            pltpu.VMEM((ROWS, D), BF16),
            pltpu.SemaphoreType.DMA((2 + 2 * PARTS,)),
        ],
        compiler_params=pltpu.CompilerParams(vmem_limit_bytes=32 * 2**20),
        name="finish",
    )(*parts)
    return query_loss.reshape(ROWS), response_loss.reshape(ROWS), query_grad, response_grad


def solution(mesh):
    both = ("wide", "narrow")
    return jax.shard_map(
        shards,
        mesh=mesh,
        in_specs=(P(both, None), P(both, None), P()),
        out_specs=(P(both), P(both), P(both, None), P(both, None)),
        check_vma=False,
    )
```
